512 devices in a mesh: pole: 16 (over x, z_hi), leaf: 32 (over y, z_lo, core).
Axes of the slice: x: 4, y: 4, z: 16 (z_hi: 4, z_lo: 4; z = z_hi * 4 + z_lo), core: 2. Of those that a mesh axis runs over, the one named last changes fastest.
Arguments:
- root_inverse: bfloat16 [16, 2, 2048, 2048], P('pole', None, 'leaf'), may hold values from -6 to 6
- factor_child: bfloat16 [16, 2, 192, 4096], P('pole', None, None, 'leaf'), may hold values from -0.3125 to 0.3125
- factor_grand: bfloat16 [16, 2, 192, 8192], P('pole', None, None, 'leaf'), may hold values from -0.3125 to 0.3125
- diag_child: bfloat16 [16, 2, 2048, 4096], P('pole', None, None, 'leaf'), may hold values from -6 to 6
- diag_grand: bfloat16 [16, 2, 2048, 8192], P('pole', None, None, 'leaf'), may hold values from -6 to 6
- struct_child: int32 [2, 192], replicated, may hold values from 0 to 2047, as said below
- struct_grand: int32 [4, 192], replicated, may hold values from 0 to 2239, as said below
- pole_weight: float32 [16, 2], P('pole'), may hold values from -1.5 to 1.5
Outputs:
- density_child: float32 [2048, 4096], P('pole', 'leaf')
- density_grand: float32 [2048, 8192], P('pole', 'leaf')
The draws below stay inside these ranges and needn't reach their ends.
Inputs may be any that keep to these rules, and one draw needn't show every extreme that they name: `struct_child`: each row holds 192 distinct increasing indices of the root separator's 2048 rows. `struct_grand`: each row holds 192 distinct increasing indices: the first half below 2048 (rows of the parent separator), the second half from 2048 on (the parent's structure rows).
All inputs are finite; a program needn't handle non-finite values.
Results may differ from the reference program's by a relative error of at most 0.004.
Values may be sent and summed in bfloat16 or wider, within the bound.
A program may use at most 64 MiB of HBM per device.

```python
import jax
import jax.numpy as jnp
from jax import lax

S = 2048
M = 192
POLES = 16


def draw_struct_child(key, part):
    key = jax.random.fold_in(key, 11)
    rows_list = []
    for child_index in range(2):
        sub_key = jax.random.fold_in(key, child_index)
        rows_list.append(jnp.sort(jax.random.permutation(sub_key, S)[:M]))
    return jnp.stack(rows_list).astype(jnp.int32)


def draw_struct_grand(key, part):
    key = jax.random.fold_in(key, 12)
    rows_list = []
    for grand_index in range(4):
        sub_key = jax.random.fold_in(key, grand_index)
        key_lower, key_upper = jax.random.split(sub_key)
        lower_rows = jnp.sort(jax.random.permutation(key_lower, S)[:M // 2])
        upper_rows = S + jnp.sort(jax.random.permutation(key_upper, M)[:M // 2])
        rows_list.append(jnp.concatenate([lower_rows, upper_rows]))
    return jnp.stack(rows_list).astype(jnp.int32)


def strengthened(result, rng, source, target, blocks, factor):
    def block_of(dim):
        return (jnp.arange(result.shape[dim]) // (result.shape[dim] // blocks)).reshape((-1,) + (1,) * (result.ndim - 1 - dim))

    one_side = jax.random.permutation(rng, blocks)[block_of(target)]
    far = (block_of(target) + blocks // 2) % blocks
    return jnp.where((block_of(source) == one_side) | (block_of(source) == far), factor * result, result)


def steps_of(stream_key, dims, shards, low, top_value):
    factor_of, own = 1.0, jax.random.fold_in(stream_key, 6)
    for axis_at, parts in shards:
        heights = jnp.exp(jax.random.uniform(jax.random.fold_in(own, axis_at), (parts,), jnp.float32, low / len(shards), top_value / len(shards)))
        factor_of = factor_of * jnp.repeat(heights, dims[axis_at] // parts).reshape([-1 if axis == axis_at else 1 for axis in range(len(dims))])
    return factor_of


def normal_values(stream_key, shape, width, reach, cuts=(), held_as=jnp.bfloat16):
    drawn = jax.random.normal(stream_key, shape, jnp.float32) * width
    if len(cuts) > 0:
        drawn = steps_of(stream_key, shape, cuts, -0.22, 0.18) * drawn
    return jnp.clip(drawn, min=-reach, max=reach).astype(held_as)


def gaussian_with(rng, shape, spread, most, cuts, heavy, held_as=jnp.bfloat16):
    array = spread * jax.random.normal(rng, shape, jnp.float32)
    if cuts:
        array = array * steps_of(rng, shape, cuts, -0.22, 0.18)
    return jnp.clip(strengthened(array, jax.random.fold_in(rng, 3), *heavy), -most, most).astype(held_as)


def setup_inputs(seed: int = 0) -> dict:
    streams_of = jax.random.split(jax.random.key(seed), 9)
    return {
        "root_inverse": normal_values(streams_of[0], (POLES, 2, S, S), 1.0, 6.0, ((0, 16), (2, 32))),
        "factor_child": normal_values(streams_of[1], (POLES, 2, M, 2 * S), (2 * M) ** -0.5, 0.3125, ((0, 16), (3, 32))),
        "factor_grand": normal_values(streams_of[2], (POLES, 2, M, 4 * S), (2 * M) ** -0.5, 0.3125, ((0, 16), (3, 32))),
        "diag_child": gaussian_with(streams_of[3], (POLES, 2, S, 2 * S), 1.0, 6.0, ((0, 16), (3, 32)), (0, 2, 16, 2.0)),
        "diag_grand": gaussian_with(streams_of[4], (POLES, 2, S, 4 * S), 1.0, 6.0, ((0, 16), (3, 32)), (0, 2, 16, 2.0)),
        "struct_child": draw_struct_child(jax.random.fold_in(streams_of[8], 71), 0),
        "struct_grand": draw_struct_grand(jax.random.fold_in(streams_of[8], 71), 0),
        "pole_weight": normal_values(streams_of[7], (POLES, 2), 0.25, 1.5, ((0, 16),), jnp.float32),
    }


def complex_product(left_real, left_imag, right_real, right_imag):
    real_part = jnp.dot(left_real, right_real, preferred_element_type=jnp.float32) - jnp.dot(left_imag, right_imag, preferred_element_type=jnp.float32)
    imag_part = jnp.dot(left_real, right_imag, preferred_element_type=jnp.float32) + jnp.dot(left_imag, right_real, preferred_element_type=jnp.float32)
    return jnp.stack([real_part, imag_part])


def solve_reference(ancestor, factor, diagonal):
    offdiag = (-complex_product(ancestor[0], ancestor[1], factor[0], factor[1])).astype(jnp.bfloat16)
    reduced = complex_product(factor[0].T, factor[1].T, offdiag[0], offdiag[1])
    inverse_block = (diagonal.astype(jnp.float32) - reduced).astype(jnp.bfloat16)
    return offdiag, inverse_block


def select_block(matrix, picked):
    return jnp.take(jnp.take(matrix, picked, axis=1), picked, axis=2)


def one_pole(root_block, child_factors, grand_factors, child_diags, grand_diags, struct_child, struct_grand):
    order = root_block.shape[1]
    child_blocks = []
    grand_blocks = []
    for child_index in range(2):
        ancestor = select_block(root_block, struct_child[child_index])
        factor = child_factors[:, :, child_index * order:(child_index + 1) * order]
        diagonal = child_diags[:, :, child_index * order:(child_index + 1) * order]
        offdiag, inverse_block = solve_reference(ancestor, factor, diagonal)
        child_blocks.append(inverse_block)
        upper = jnp.concatenate([inverse_block, jnp.transpose(offdiag, (0, 2, 1))], axis=2)
        lower = jnp.concatenate([offdiag, ancestor], axis=2)
        extended = jnp.concatenate([upper, lower], axis=1)
        for grand_offset in range(2):
            grand_index = 2 * child_index + grand_offset
            nested = select_block(extended, struct_grand[grand_index])
            factor_two = grand_factors[:, :, grand_index * order:(grand_index + 1) * order]
            diagonal_two = grand_diags[:, :, grand_index * order:(grand_index + 1) * order]
            unused_off, grand_block = solve_reference(nested, factor_two, diagonal_two)
            grand_blocks.append(grand_block)
    return jnp.concatenate(child_blocks, axis=2), jnp.concatenate(grand_blocks, axis=2)


def reference(root_inverse, factor_child, factor_grand, diag_child, diag_grand, struct_child, struct_grand, pole_weight):
    def accumulate(carry, inputs):
        root_block, child_factors, grand_factors, child_diags, grand_diags, weight = inputs
        child_all, grand_all = one_pole(root_block, child_factors, grand_factors, child_diags, grand_diags, struct_child, struct_grand)
        child_term = weight[0] * child_all[1].astype(jnp.float32) + weight[1] * child_all[0].astype(jnp.float32)
        grand_term = weight[0] * grand_all[1].astype(jnp.float32) + weight[1] * grand_all[0].astype(jnp.float32)
        return (carry[0] + child_term, carry[1] + grand_term), None

    order = root_inverse.shape[2]
    start = (jnp.zeros((order, 2 * order), jnp.float32), jnp.zeros((order, 4 * order), jnp.float32))
    summed, unused = lax.scan(accumulate, start, (root_inverse, factor_child, factor_grand, diag_child, diag_grand, pole_weight))
    return summed[0], summed[1]
```

```python
import jax
import jax.numpy as jnp
from jax import lax
from jax.experimental import pallas as pl
from jax.experimental.pallas import tpu as pltpu
from jax.sharding import PartitionSpec as P

MESH = pl.DeviceIdType.MESH
BF = jnp.bfloat16
F32 = jnp.float32


def mm(a, b):
    return jnp.dot(a, b, preferred_element_type=F32)


def mm_nt(a, b):
    return lax.dot_general(a, b, (((1,), (1,)), ((), ())), preferred_element_type=F32)


def hot(cond):
    return jnp.where(cond, 1.0, 0.0).astype(BF)


def column(row):
    return jnp.transpose(jnp.broadcast_to(row.astype(F32), (128, 128)))


def iota(shape, dim):
    return lax.broadcasted_iota(jnp.int32, shape, dim).astype(F32)


def twice(row):
    return jnp.concatenate([row, row], axis=1)


def row_of(ref, index, lanes):
    row = ref[0:1, lanes]
    for i in range(1, ref.shape[0]):
        row = jnp.where(index == i, ref[i : i + 1, lanes], row)
    return row


def right_side(off_re, off_im):
    re_col = jnp.concatenate([off_re[:128], -off_im[:128], off_re[128:], -off_im[128:]], axis=0)
    im_col = jnp.concatenate([off_im[:128], off_re[:128], off_im[128:], off_re[128:]], axis=0)
    return re_col, im_col


def transposed(ref, cols):
    parts = [
        ref[0, 0:128, cols],
        ref[1, 0:128, cols],
        jnp.concatenate([ref[0, 128:192, cols], ref[1, 128:192, cols]], axis=0),
    ]
    return jnp.concatenate([jnp.transpose(p.astype(F32)) for p in parts], axis=1).astype(BF)


def kernel(
    root,
    fc,
    fg,
    dc,
    dg,
    sc,
    sg,
    pw,
    out_c,
    out_g,
    root_v,
    fc_v,
    fg_v,
    dc_v,
    dg_v,
    ftc,
    ftg,
    oh,
    rl,
    t_send,
    t_recv,
    d_send,
    d_recv,
    part,
    rs_recv,
    full,
    acat,
    agcat,
    rhs_c,
    rhs_g,
    sx_c,
    sx_g,
    rx_c,
    rx_g,
    sz_c,
    sz_g,
    rz_c,
    rz_g,
    lsem,
    ty_s,
    ty_r,
    dy_s,
    dy_r,
    e3_s,
    e3_r,
    e4_s,
    e4_r,
    cz_s,
    cz_r,
    cy_s,
    cy_r,
    cc_s,
    cc_r,
    gz_s,
    gz_r,
    gc_s,
    gc_r,
    xc_s,
    xc_r,
    xg_s,
    xg_r,
    zc_s,
    zc_r,
    zg_s,
    zg_r,
):
    p = lax.axis_index("pole")
    leaf = lax.axis_index("leaf")
    x = p // 4
    zh = p % 4
    y = leaf // 8
    e = leaf % 8
    zl = e // 2
    k = e % 2
    c = y // 2
    yp = y % 2
    y_mate = y + 1 - 2 * yp
    base = y * 8

    def copy(src, dst, ssem, rsem, pole_to, leaf_to):
        return pltpu.make_async_remote_copy(
            src_ref=src,
            dst_ref=dst,
            send_sem=ssem,
            recv_sem=rsem,
            device_id=(pole_to, leaf_to),
            device_id_type=MESH,
        )

    def arrived(dst, rsem):
        copy(dst, dst, rsem, rsem, p, leaf).wait_recv()

    def sent(src, ssem):
        copy(src, src, ssem, ssem, p, leaf).wait_send()

    barrier = pltpu.get_barrier_semaphore()

    def greet(pole_to, leaf_to):
        pl.semaphore_signal(barrier, inc=1, device_id=(pole_to, leaf_to), device_id_type=MESH)

    for t in range(1, 4):
        greet(p, (y + t) % 4 * 8 + e)
        greet((x + t) % 4 * 4 + zh, leaf)
        greet(x * 4 + (zh + t) % 4, leaf)
    for t in range(1, 8):
        greet(p, base + (e + t) % 8)

    loads = [
        pltpu.make_async_copy(root.at[0, 0], root_v.at[0:64], lsem.at[0]),
        pltpu.make_async_copy(root.at[0, 1], root_v.at[64:128], lsem.at[1]),
        pltpu.make_async_copy(fc.at[0], fc_v, lsem.at[2]),
        pltpu.make_async_copy(fg.at[0], fg_v, lsem.at[3]),
        pltpu.make_async_copy(dc.at[0, 0], dc_v.at[:, 0:128], lsem.at[4]),
        pltpu.make_async_copy(dc.at[0, 1], dc_v.at[:, 128:256], lsem.at[5]),
        pltpu.make_async_copy(dg.at[0, 0], dg_v.at[:, 0:256], lsem.at[6]),
        pltpu.make_async_copy(dg.at[0, 1], dg_v.at[:, 256:512], lsem.at[7]),
    ]
    for load in loads:
        load.start()

    own_c = pl.multiple_of((yp * 8 + e) * 128, 128)
    own_g = pl.multiple_of(e * 256, 256)
    loads[2].wait()
    ftc[pl.ds(own_c, 128), :] = transposed(fc_v, slice(0, 128))
    loads[3].wait()
    ftg[pl.ds(own_g, 128), :] = transposed(fg_v, slice(0, 128))
    ftg[pl.ds(pl.multiple_of(own_g + 128, 128), 128), :] = transposed(fg_v, slice(128, 256))

    child_rows = [sc[0:1, 0:128], twice(sc[0:1, 128:192]), sc[1:2, 0:128], twice(sc[1:2, 128:192])]
    hot_rows = jnp.concatenate(child_rows, axis=1).astype(F32)

    def build_hot(i, carry):
        at = pl.multiple_of(i * 128, 128)
        ids = iota((128, 512), 0) + (i * 128).astype(F32)
        oh[pl.ds(at, 128), :] = hot(ids == hot_rows)
        return carry

    lax.fori_loop(0, 16, build_hot, 0)
    loads[0].wait()
    loads[1].wait()
    taken = mm(root_v[...], oh[...])
    low_lanes = iota((64, 128), 1) < 64
    for ch in range(2):
        at = ch * 256
        t_send[ch, 0:64, :] = taken[0:64, at : at + 128].astype(BF)
        t_send[ch, 64:128, :] = taken[64:128, at : at + 128].astype(BF)
        t_send[ch, 128:192, :] = jnp.where(
            low_lanes, taken[0:64, at + 128 : at + 256], taken[64:128, at + 128 : at + 256]
        ).astype(BF)

    pl.semaphore_wait(barrier, 16)

    for t in range(1, 4):
        y_to = (y + t) % 4
        copy(t_send.at[y_to // 2], t_recv.at[y], ty_s.at[t - 1], ty_r.at[y], p, y_to * 8 + e).start()
    t_recv[pl.ds(y, 1)] = t_send[pl.ds(c, 1)]

    def c_block(yy, j, kk):
        return ftc.at[pl.ds(pl.multiple_of((yy * 8 + j * 2 + kk) * 128, 128), 128)]

    def g_block(j, kk):
        return ftg.at[pl.ds(pl.multiple_of((j * 2 + kk) * 256, 256), 256)]

    def c_up(j):
        return copy(c_block(yp, j, k), c_block(yp, j, k), cz_s.at[j], cz_r.at[j], p, base + e + 2)

    def c_down(j):
        return copy(c_block(yp, j, k), c_block(yp, j, k), cz_s.at[4 + j], cz_r.at[j], p, base + e - 2)

    def c_side(j):
        return copy(c_block(yp, j, k), c_block(yp, j, k), cy_s.at[j], cy_r.at[j], p, y_mate * 8 + e)

    def c_core(yy, j):
        i = yy * 4 + j
        return copy(c_block(yy, j, k), c_block(yy, j, k), cc_s.at[i], cc_r.at[i], p, base + e + 1 - 2 * k)

    def g_up(j):
        return copy(g_block(j, k), g_block(j, k), gz_s.at[j], gz_r.at[j], p, base + e + 2)

    def g_down(j):
        return copy(g_block(j, k), g_block(j, k), gz_s.at[4 + j], gz_r.at[j], p, base + e - 2)

    def g_core(j):
        return copy(g_block(j, k), g_block(j, k), gc_s.at[j], gc_r.at[j], p, base + e + 1 - 2 * k)

    @pl.when(zl < 3)
    def _():
        c_up(zl).start()

    @pl.when(zl > 0)
    def _():
        c_down(zl).start()

    c_side(zl).start()
    c_core(yp, zl).start()

    @pl.when(zl < 3)
    def _():
        g_up(zl).start()

    @pl.when(zl > 0)
    def _():
        g_down(zl).start()

    g_core(zl).start()

    def c_relay(s):
        @pl.when(zl >= s)
        def _():
            j = zl - s
            arrived(c_block(yp, j, k), cz_r.at[j])

            @pl.when(zl < 3)
            def _():
                c_up(j).start()

            c_side(j).start()
            c_core(yp, j).start()

        @pl.when(zl + s <= 3)
        def _():
            j = zl + s
            arrived(c_block(yp, j, k), cz_r.at[j])

            @pl.when(zl > 0)
            def _():
                c_down(j).start()

            c_side(j).start()
            c_core(yp, j).start()

    def g_relay(s):
        @pl.when(zl >= s)
        def _():
            j = zl - s
            arrived(g_block(j, k), gz_r.at[j])

            @pl.when(zl < 3)
            def _():
                g_up(j).start()

            g_core(j).start()

        @pl.when(zl + s <= 3)
        def _():
            j = zl + s
            arrived(g_block(j, k), gz_r.at[j])

            @pl.when(zl > 0)
            def _():
                g_down(j).start()

            g_core(j).start()

    col0 = column(row_of(sg, y, slice(0, 128)))
    col1 = column(twice(row_of(sg, y, slice(128, 192))))
    col_mate = column(row_of(sg, y_mate, slice(0, 128)))
    lane = iota((128, 128), 1)

    def build_low(i, carry):
        at = pl.multiple_of(i * 128, 128)
        ids = lane + (i * 128).astype(F32)
        rl[0:128, pl.ds(at, 128)] = hot(col0 == ids)
        rl[128:256, pl.ds(at, 128)] = hot(col_mate == ids)
        return carry

    lax.fori_loop(0, 16, build_low, 0)
    loads[4].wait()
    loads[5].wait()
    picked = mm(rl[...], dc_v[...]).astype(BF)
    own_ids = iota((128, 128), 0) + own_c.astype(F32)
    pick_own = hot(own_ids == row_of(sg, y, slice(0, 128)).astype(F32))
    pick_mate = hot(own_ids == row_of(sg, y_mate, slice(0, 128)).astype(F32))
    d_send[0:96, :] = mm(picked[128:224, 0:128], pick_mate).astype(BF)
    d_send[96:192, :] = mm(picked[128:224, 128:256], pick_mate).astype(BF)
    copy(d_send, d_recv, dy_s.at[0], dy_r.at[0], p, y_mate * 8 + e).start()
    d_re = mm(picked[0:96, 0:128], pick_own)
    d_im = mm(picked[0:96, 128:256], pick_own)

    a_row0 = column(row_of(sc, c, slice(0, 128)))
    a_row1 = column(twice(row_of(sc, c, slice(128, 192))))
    lane_at = jnp.where(lane < 64, lane, lane + 448.0) + (e * 64).astype(F32)
    fold = jnp.concatenate(
        [
            jnp.concatenate([hot(a_row0 == lane_at), hot(a_row0 == lane_at + 1024.0)], axis=1),
            jnp.concatenate([hot(a_row1 == lane_at), hot(a_row1 == lane_at + 1024.0)], axis=1)[0:64],
        ],
        axis=0,
    )
    for t in range(1, 4):
        y_from = (y + t) % 4
        arrived(t_recv.at[y_from], ty_r.at[y_from])
    for b in range(3):
        raw = jnp.concatenate([t_recv[i, b * 64 : b * 64 + 64, :] for i in range(4)], axis=0)
        part[b * 192 : b * 192 + 192, :] = mm(fold, raw).astype(BF)
    arrived(d_recv, dy_r.at[0])
    part[576:672, :] = (d_re + d_recv[0:96, :].astype(F32)).astype(BF)
    part[672:768, :] = (d_im + d_recv[96:192, :].astype(F32)).astype(BF)

    def piece(ref, i):
        return ref.at[pl.ds(pl.multiple_of(i * 96, 96), 96)]

    for t in range(1, 8):
        to = (e + t) % 8
        copy(piece(part, to), rs_recv.at[e], e3_s.at[t - 1], e3_r.at[e], p, base + to).start()
    c_relay(1)
    total = part[pl.ds(pl.multiple_of(e * 96, 96), 96), :].astype(F32)
    for t in range(1, 8):
        at = (e + t) % 8
        arrived(rs_recv.at[at], e3_r.at[at])
        total = total + rs_recv[at].astype(F32)
    full[pl.ds(pl.multiple_of(e * 96, 96), 96), :] = total.astype(BF)

    for t in range(1, 8):
        to = (e + t) % 8
        copy(piece(full, e), piece(full, e), e4_s.at[t - 1], e4_r.at[e], p, base + to).start()
    c_relay(2)
    g_relay(1)
    for t in range(1, 8):
        at = (e + t) % 8
        arrived(piece(full, at), e4_r.at[at])
    for b in range(3):
        acat[:, b * 128 : b * 128 + 128] = full[b * 192 : b * 192 + 192, :]

    g_re, g_im = right_side(fc_v[0], fc_v[1])
    a_now = acat[...]
    off_re = (-mm(a_now, g_re)).astype(BF)
    off_im = (-mm(a_now, g_im)).astype(BF)
    r_re, r_im = right_side(off_re, off_im)
    rhs_c[:, 0:128] = r_re
    rhs_c[:, 128:256] = r_im

    c_relay(3)
    for i in range(4):
        arrived(c_block(1 - yp, i, k), cy_r.at[i])
        c_core(1 - yp, i).start()
    for i in range(8):
        arrived(c_block(i // 4, i % 4, 1 - k), cc_r.at[i])

    ft_r = mm(rl[0:128, :], ftc[...])
    lane384 = lax.broadcasted_iota(jnp.int32, (128, 384), 1)
    is_im = ((lane384 >= 128) & (lane384 < 256)) | (lane384 >= 320)
    f_re = jnp.where(is_im, -ft_r, ft_r).astype(BF)
    f_im = jnp.concatenate(
        [ft_r[:, 128:256], ft_r[:, 0:128], pltpu.roll(ft_r[:, 256:384], 64, 1)], axis=1
    ).astype(BF)
    a_low = acat[0:128, :]
    a_high = jnp.concatenate([acat[128:192, :], acat[128:192, :]], axis=0)
    off_t = jnp.concatenate(
        [
            -mm_nt(f_re, a_low),
            -mm_nt(f_im, a_low),
            -jnp.where(lane < 64, mm_nt(f_re, a_high), mm_nt(f_im, a_high)),
        ],
        axis=1,
    ).astype(BF)
    none = jnp.zeros((128, 128), BF)
    up0 = col0 - 2048.0
    up1 = col1 - 2048.0
    lane_hi = jnp.where(lane < 64, lane, lane - 64.0) + 128.0
    near0 = hot(up0 == lane)
    near1 = hot(up1 == lane)
    far0 = up0 == lane_hi
    far1 = up1 == lane_hi
    sub = iota((128, 128), 0)
    q0 = jnp.concatenate([near0, none, hot(far0 & (lane < 64))], axis=1)
    q1 = jnp.concatenate([none, near0, hot(far0 & (lane >= 64))], axis=1)
    q2 = jnp.concatenate(
        [
            jnp.where(sub < 64, near1.astype(F32), 0.0).astype(BF),
            jnp.where(sub >= 64, near1.astype(F32), 0.0).astype(BF),
            hot(far1 & ((lane < 64) == (sub < 64))),
        ],
        axis=1,
    )
    up_near = jnp.concatenate([near0, near1[0:64]], axis=0)
    up_far = jnp.concatenate([hot(far0), hot(far1)[0:64]], axis=0)[:, 0:64]
    a_rows = mm(up_near, acat[0:128, :]) + mm(up_far, acat[128:192, :])
    rows_all = a_rows + jnp.concatenate([off_t.astype(F32), jnp.zeros((64, 384), F32)], axis=0)
    q_all = jnp.concatenate([q0, q1, q2], axis=0)
    ag = mm_nt(rows_all.astype(BF), q_all)
    up_re = jnp.concatenate([q0, q2[0:64]], axis=0)
    up_im = jnp.concatenate([q1, q2[64:128]], axis=0)
    rest = jnp.zeros((32, 128), F32)
    tail = jnp.zeros((64, 128), F32)
    in_re = jnp.concatenate([full[576:672, :].astype(F32), rest], axis=0) - mm_nt(f_re, off_t)
    in_im = jnp.concatenate([full[672:768, :].astype(F32), rest], axis=0) - mm_nt(f_im, off_t)
    agcat[:, 0:128] = (
        ag[:, 0:128] + mm_nt(up_re, off_t) + jnp.concatenate([in_re, tail], axis=0)
    ).astype(BF)
    agcat[:, 128:256] = (
        ag[:, 128:256] + mm_nt(up_im, off_t) + jnp.concatenate([in_im, tail], axis=0)
    ).astype(BF)
    agcat[:, 256:384] = ag[:, 256:384].astype(BF)

    g_relay(2)

    gg_re, gg_im = right_side(fg_v[0], fg_v[1])
    ag_now = agcat[...]
    goff_re = (-mm(ag_now, gg_re)).astype(BF)
    goff_im = (-mm(ag_now, gg_im)).astype(BF)
    r_re, r_im = right_side(goff_re, goff_im)
    rhs_g[:, 0:256] = r_re
    rhs_g[:, 256:512] = r_im

    w_im = pw[0, 0]
    w_re = pw[0, 1]

    def density(acc, diag, n):
        re = (diag[:, 0:n].astype(F32) - acc[:, 0:n]).astype(BF).astype(F32)
        im = (diag[:, n : 2 * n].astype(F32) - acc[:, n : 2 * n]).astype(BF).astype(F32)
        return (w_im * im + w_re * re).astype(BF)

    for t in range(1, 5):
        x_to = (x + t) % 4

        def c_rows(i, carry, x_to=x_to):
            at = pl.multiple_of(i * 256, 256)
            rows = pl.ds(pl.multiple_of(x_to * 512 + i * 256, 256), 256)
            sx_c[x_to, pl.ds(at, 256), :] = density(mm(ftc[rows, :], rhs_c[...]), dc_v[rows, :], 128)
            return carry

        lax.fori_loop(0, 2, c_rows, 0)
        if t < 4:
            copy(sx_c.at[x_to], rx_c.at[x], xc_s.at[t - 1], xc_r.at[x], x_to * 4 + zh, leaf).start()

    g_relay(3)
    for i in range(4):
        arrived(g_block(i, 1 - k), gc_r.at[i])
    loads[6].wait()
    loads[7].wait()

    for t in range(1, 5):
        x_to = (x + t) % 4

        def g_rows(i, carry, x_to=x_to):
            at = pl.multiple_of(i * 256, 256)
            rows = pl.ds(pl.multiple_of(x_to * 512 + i * 256, 256), 256)
            sx_g[x_to, pl.ds(at, 256), :] = density(mm(ftg[rows, :], rhs_g[...]), dg_v[rows, :], 256)
            return carry

        lax.fori_loop(0, 2, g_rows, 0)
        if t < 4:
            copy(sx_g.at[x_to], rx_g.at[x], xg_s.at[t - 1], xg_r.at[x], x_to * 4 + zh, leaf).start()

    def along_z(sx, rx, sz, rz, xr, zs, zr):
        for t in range(1, 4):
            x_from = (x + t) % 4
            arrived(rx.at[x_from], xr.at[x_from])
        for t in range(1, 5):
            to = (zh + t) % 4
            rows = pl.ds(pl.multiple_of(to * 128, 128), 128)
            total = sx[x, rows, :].astype(F32)
            for u in range(1, 4):
                total = total + rx[(x + u) % 4, rows, :].astype(F32)
            if t < 4:
                sz[to] = total.astype(BF)
                copy(sz.at[to], rz.at[zh], zs.at[t - 1], zr.at[zh], x * 4 + to, leaf).start()
        return total

    own_cs = along_z(sx_c, rx_c, sz_c, rz_c, xc_r, zc_s, zc_r)
    own_gs = along_z(sx_g, rx_g, sz_g, rz_g, xg_r, zg_s, zg_r)
    for t in range(1, 4):
        z_from = (zh + t) % 4
        arrived(rz_c.at[z_from], zc_r.at[z_from])
        own_cs = own_cs + rz_c[z_from].astype(F32)
    out_c[...] = own_cs
    for t in range(1, 4):
        z_from = (zh + t) % 4
        arrived(rz_g.at[z_from], zg_r.at[z_from])
        own_gs = own_gs + rz_g[z_from].astype(F32)
    out_g[...] = own_gs

    for t in range(3):
        sent(t_send.at[0], ty_s.at[t])
        sent(sx_c.at[0], xc_s.at[t])
        sent(sx_g.at[0], xg_s.at[t])
        sent(sz_c.at[0], zc_s.at[t])
        sent(sz_g.at[0], zg_s.at[t])
    sent(d_send, dy_s.at[0])
    for t in range(7):
        sent(piece(part, 0), e3_s.at[t])
        sent(piece(full, 0), e4_s.at[t])
    for j in range(4):

        @pl.when((zl < 3) & (j <= zl))
        def _(j=j):
            sent(c_block(0, 0, 0), cz_s.at[j])
            sent(g_block(0, 0), gz_s.at[j])

        @pl.when((zl > 0) & (j >= zl))
        def _(j=j):
            sent(c_block(0, 0, 0), cz_s.at[4 + j])
            sent(g_block(0, 0), gz_s.at[4 + j])

        sent(c_block(0, 0, 0), cy_s.at[j])
        sent(c_block(0, 0, 0), cc_s.at[j])
        sent(c_block(0, 0, 0), cc_s.at[4 + j])
        sent(g_block(0, 0), gc_s.at[j])


def local(*args):
    vm = pltpu.VMEM
    dma = pltpu.SemaphoreType.DMA
    scratch = [
        vm((128, 2048), BF),
        vm((2, 192, 128), BF),
        vm((2, 192, 256), BF),
        vm((2048, 256), BF),
        vm((2048, 512), BF),
        vm((2048, 384), BF),
        vm((2048, 384), BF),
        vm((2048, 512), BF),
        vm((256, 2048), BF),
        vm((2, 192, 128), BF),
        vm((4, 192, 128), BF),
        vm((192, 128), BF),
        vm((192, 128), BF),
        vm((768, 128), BF),
        vm((8, 96, 128), BF),
        vm((768, 128), BF),
        vm((192, 384), BF),
        vm((192, 384), BF),
        vm((384, 256), BF),
        vm((384, 512), BF),
        vm((4, 512, 128), BF),
        vm((4, 512, 256), BF),
        vm((4, 512, 128), BF),
        vm((4, 512, 256), BF),
        vm((4, 128, 128), BF),
        vm((4, 128, 256), BF),
        vm((4, 128, 128), BF),
        vm((4, 128, 256), BF),
        dma((8,)),
        dma((3,)),
        dma((4,)),
        dma((1,)),
        dma((1,)),
        dma((7,)),
        dma((8,)),
        dma((7,)),
        dma((8,)),
        dma((8,)),
        dma((4,)),
        dma((4,)),
        dma((4,)),
        dma((8,)),
        dma((8,)),
        dma((8,)),
        dma((4,)),
        dma((4,)),
        dma((4,)),
        dma((3,)),
        dma((4,)),
        dma((3,)),
        dma((4,)),
        dma((3,)),
        dma((4,)),
        dma((3,)),
        dma((4,)),
    ]
    any_spec = pl.BlockSpec(memory_space=pl.ANY)
    vm_spec = pl.BlockSpec(memory_space=pltpu.VMEM)
    return pl.pallas_call(
        kernel,
        out_shape=[
            jax.ShapeDtypeStruct((128, 128), F32),
            jax.ShapeDtypeStruct((128, 256), F32),
        ],
        in_specs=[any_spec] * 5 + [vm_spec] * 2 + [pl.BlockSpec(memory_space=pltpu.SMEM)],
        out_specs=[vm_spec, vm_spec],
        scratch_shapes=scratch,
        compiler_params=pltpu.CompilerParams(
            collective_id=0, has_side_effects=True, vmem_limit_bytes=40 * 1024 * 1024
        ),
        cost_estimate=pl.CostEstimate(flops=3_000_000_000, bytes_accessed=5_000_000, transcendentals=0),
    )(*args)


def solution(mesh):
    placed = (
        P("pole", None, "leaf", None),
        P("pole", None, None, "leaf"),
        P("pole", None, None, "leaf"),
        P("pole", None, None, "leaf"),
        P("pole", None, None, "leaf"),
        P(),
        P(),
        P("pole", None),
    )
    return jax.shard_map(
        local,
        mesh=mesh,
        in_specs=placed,
        out_specs=(P("pole", "leaf"), P("pole", "leaf")),
        check_vma=False,
    )
```

```python
import jax
import jax.numpy as jnp
from jax import lax
from jax.experimental import pallas as pl
from jax.experimental.pallas import tpu as pltpu
from jax.sharding import PartitionSpec as P

MESH = pl.DeviceIdType.MESH
BF = jnp.bfloat16
F32 = jnp.float32


def mm(a, b):
    return jnp.dot(a, b, preferred_element_type=F32)


def mm_nt(a, b):
    return lax.dot_general(a, b, (((1,), (1,)), ((), ())), preferred_element_type=F32)


def hot(cond):
    return jnp.where(cond, 1.0, 0.0).astype(BF)


def column(row):
    return jnp.transpose(jnp.broadcast_to(row.astype(F32), (128, 128)))


def iota(shape, dim):
    return lax.broadcasted_iota(jnp.int32, shape, dim).astype(F32)


def twice(row):
    return jnp.concatenate([row, row], axis=1)


def row_of(ref, index, lanes):
    row = ref[0:1, lanes]
    for i in range(1, ref.shape[0]):
        row = jnp.where(index == i, ref[i : i + 1, lanes], row)
    return row


def right_side(off_re, off_im):
    re_col = jnp.concatenate([off_re[:128], -off_im[:128], off_re[128:], -off_im[128:]], axis=0)
    im_col = jnp.concatenate([off_im[:128], off_re[:128], off_im[128:], off_re[128:]], axis=0)
    return re_col, im_col


def transposed(ref, cols):
    parts = [
        ref[0, 0:128, cols],
        ref[1, 0:128, cols],
        jnp.concatenate([ref[0, 128:192, cols], ref[1, 128:192, cols]], axis=0),
    ]
    return jnp.concatenate([jnp.transpose(p.astype(F32)) for p in parts], axis=1).astype(BF)


def kernel(
    root,
    fc,
    fg,
    dc,
    dg,
    sc_hbm,
    sg_hbm,
    pw_hbm,
    out_c,
    out_g,
    sc,
    sg,
    pw,
    root_v,
    fc_v,
    fg_v,
    diag_v,
    ftc,
    ftg,
    oh,
    rl,
    t_send,
    t_recv,
    d_send,
    d_recv,
    part,
    rs_recv,
    full,
    acat,
    agcat,
    rhs,
    s_opp,
    r_opp,
    s_nb,
    r_nb,
    own,
    sz,
    rz,
    keep,
    lsem,
    ty_s,
    ty_r,
    dy_s,
    dy_r,
    e3_s,
    e3_r,
    e4_s,
    e4_r,
    cz_s,
    cz_r,
    cy_s,
    cy_r,
    cc_s,
    cc_r,
    gz_s,
    gz_r,
    gc_s,
    gc_r,
    op_s,
    op_r,
    nb_s,
    nb_r,
    z_s,
    z_r,
):
    p = lax.axis_index("pole")
    leaf = lax.axis_index("leaf")
    x = p // 4
    zh = p % 4
    y = leaf // 8
    e = leaf % 8
    zl = e // 2
    k = e % 2
    c = y // 2
    yp = y % 2
    y_mate = y + 1 - 2 * yp
    base = y * 8

    def copy(src, dst, ssem, rsem, pole_to, leaf_to):
        return pltpu.make_async_remote_copy(
            src_ref=src,
            dst_ref=dst,
            send_sem=ssem,
            recv_sem=rsem,
            device_id=(pole_to, leaf_to),
            device_id_type=MESH,
        )

    def arrived(dst, rsem):
        copy(dst, dst, rsem, rsem, p, leaf).wait_recv()

    def sent(src, ssem):
        copy(src, src, ssem, ssem, p, leaf).wait_send()

    barrier = pltpu.get_barrier_semaphore()

    def greet(pole_to, leaf_to):
        pl.semaphore_signal(barrier, inc=1, device_id=(pole_to, leaf_to), device_id_type=MESH)

    for t in range(1, 4):
        greet(p, (y + t) % 4 * 8 + e)
        greet((x + t) % 4 * 4 + zh, leaf)
        greet(x * 4 + (zh + t) % 4, leaf)
    for t in range(1, 8):
        greet(p, base + (e + t) % 8)

    loads = [
        pltpu.make_async_copy(root.at[0, 0], root_v.at[0:64], lsem.at[0]),
        pltpu.make_async_copy(root.at[0, 1], root_v.at[64:128], lsem.at[1]),
        pltpu.make_async_copy(fc.at[0], fc_v, lsem.at[2]),
        pltpu.make_async_copy(fg.at[0], fg_v, lsem.at[3]),
        pltpu.make_async_copy(dc.at[0, 0], diag_v.at[0, :, 0:128], lsem.at[4]),
        pltpu.make_async_copy(dc.at[0, 1], diag_v.at[0, :, 128:256], lsem.at[5]),
        pltpu.make_async_copy(dg.at[0, 0, :, 0:128], diag_v.at[1, :, 0:128], lsem.at[6]),
        pltpu.make_async_copy(dg.at[0, 1, :, 0:128], diag_v.at[1, :, 128:256], lsem.at[7]),
        pltpu.make_async_copy(sc_hbm, sc, lsem.at[8]),
        pltpu.make_async_copy(sg_hbm, sg, lsem.at[9]),
        pltpu.make_async_copy(pw_hbm, pw, lsem.at[10]),
        pltpu.make_async_copy(dg.at[0, 0, :, 128:256], diag_v.at[2, :, 0:128], lsem.at[11]),
        pltpu.make_async_copy(dg.at[0, 1, :, 128:256], diag_v.at[2, :, 128:256], lsem.at[12]),
    ]
    for i in (8, 9, 2, 3, 0, 1, 4, 5, 10, 6, 7, 11, 12):
        loads[i].start()

    own_c = pl.multiple_of((yp * 8 + e) * 128, 128)
    own_g = pl.multiple_of(e * 256, 256)
    loads[2].wait()
    ftc[pl.ds(own_c, 128), :] = transposed(fc_v, slice(0, 128))
    loads[3].wait()
    ftg[pl.ds(own_g, 128), :] = transposed(fg_v, slice(0, 128))
    ftg[pl.ds(pl.multiple_of(own_g + 128, 128), 128), :] = transposed(fg_v, slice(128, 256))

    loads[8].wait()
    loads[9].wait()
    loads[10].wait()
    child_rows = [sc[0:1, 0:128], twice(sc[0:1, 128:192]), sc[1:2, 0:128], twice(sc[1:2, 128:192])]
    hot_rows = jnp.concatenate(child_rows, axis=1).astype(F32)

    def build_hot(i, carry):
        at = pl.multiple_of(i * 128, 128)
        ids = iota((128, 512), 0) + (i * 128).astype(F32)
        oh[pl.ds(at, 128), :] = hot(ids == hot_rows)
        return carry

    lax.fori_loop(0, 16, build_hot, 0)
    loads[0].wait()
    loads[1].wait()
    taken = mm(root_v[...], oh[...])
    low_lanes = iota((64, 128), 1) < 64
    for ch in range(2):
        at = ch * 256
        t_send[ch, 0:64, :] = taken[0:64, at : at + 128].astype(BF)
        t_send[ch, 64:128, :] = taken[64:128, at : at + 128].astype(BF)
        t_send[ch, 128:192, :] = jnp.where(
            low_lanes, taken[0:64, at + 128 : at + 256], taken[64:128, at + 128 : at + 256]
        ).astype(BF)

    pl.semaphore_wait(barrier, 16)

    for t in range(1, 4):
        y_to = (y + t) % 4
        copy(t_send.at[y_to // 2], t_recv.at[y], ty_s.at[t - 1], ty_r.at[y], p, y_to * 8 + e).start()
    t_recv[pl.ds(y, 1)] = t_send[pl.ds(c, 1)]

    def c_block(yy, j, kk):
        return ftc.at[pl.ds(pl.multiple_of((yy * 8 + j * 2 + kk) * 128, 128), 128)]

    def g_block(j, kk):
        return ftg.at[pl.ds(pl.multiple_of((j * 2 + kk) * 256, 256), 256)]

    def c_up(j):
        return copy(c_block(yp, j, k), c_block(yp, j, k), cz_s.at[j], cz_r.at[j], p, base + e + 2)

    def c_down(j):
        return copy(c_block(yp, j, k), c_block(yp, j, k), cz_s.at[4 + j], cz_r.at[j], p, base + e - 2)

    def c_side(j):
        return copy(c_block(yp, j, k), c_block(yp, j, k), cy_s.at[j], cy_r.at[j], p, y_mate * 8 + e)

    def c_core(yy, j):
        i = yy * 4 + j
        return copy(c_block(yy, j, k), c_block(yy, j, k), cc_s.at[i], cc_r.at[i], p, base + e + 1 - 2 * k)

    def g_up(j):
        return copy(g_block(j, k), g_block(j, k), gz_s.at[j], gz_r.at[j], p, base + e + 2)

    def g_down(j):
        return copy(g_block(j, k), g_block(j, k), gz_s.at[4 + j], gz_r.at[j], p, base + e - 2)

    def g_core(j):
        return copy(g_block(j, k), g_block(j, k), gc_s.at[j], gc_r.at[j], p, base + e + 1 - 2 * k)

    def c_first():
        @pl.when(zl < 3)
        def _():
            c_up(zl).start()

        @pl.when(zl > 0)
        def _():
            c_down(zl).start()

        c_side(zl).start()
        c_core(yp, zl).start()

    def g_first():
        @pl.when(zl < 3)
        def _():
            g_up(zl).start()

        @pl.when(zl > 0)
        def _():
            g_down(zl).start()

        g_core(zl).start()

    def c_relay(s):
        @pl.when(zl >= s)
        def _():
            j = zl - s
            arrived(c_block(yp, j, k), cz_r.at[j])

            @pl.when(zl < 3)
            def _():
                c_up(j).start()

            c_side(j).start()
            c_core(yp, j).start()

        @pl.when(zl + s <= 3)
        def _():
            j = zl + s
            arrived(c_block(yp, j, k), cz_r.at[j])

            @pl.when(zl > 0)
            def _():
                c_down(j).start()

            c_side(j).start()
            c_core(yp, j).start()

    def g_relay(s):
        @pl.when(zl >= s)
        def _():
            j = zl - s
            arrived(g_block(j, k), gz_r.at[j])

            @pl.when(zl < 3)
            def _():
                g_up(j).start()

            g_core(j).start()

        @pl.when(zl + s <= 3)
        def _():
            j = zl + s
            arrived(g_block(j, k), gz_r.at[j])

            @pl.when(zl > 0)
            def _():
                g_down(j).start()

            g_core(j).start()

    def c_finish():
        for i in range(4):
            arrived(c_block(1 - yp, i, k), cy_r.at[i])
            c_core(1 - yp, i).start()
        for i in range(8):
            arrived(c_block(i // 4, i % 4, 1 - k), cc_r.at[i])

    def g_finish():
        for i in range(4):
            arrived(g_block(i, 1 - k), gc_r.at[i])

    c_first()
    g_first()

    col0 = column(row_of(sg, y, slice(0, 128)))
    col1 = column(twice(row_of(sg, y, slice(128, 192))))
    col_mate = column(row_of(sg, y_mate, slice(0, 128)))
    lane = iota((128, 128), 1)

    def build_low(i, carry):
        at = pl.multiple_of(i * 128, 128)
        ids = lane + (i * 128).astype(F32)
        rl[0:128, pl.ds(at, 128)] = hot(col0 == ids)
        rl[128:256, pl.ds(at, 128)] = hot(col_mate == ids)
        return carry

    lax.fori_loop(0, 16, build_low, 0)
    loads[4].wait()
    loads[5].wait()
    picked = mm(rl[...], diag_v[0]).astype(BF)
    own_ids = iota((128, 128), 0) + own_c.astype(F32)
    pick_own = hot(own_ids == row_of(sg, y, slice(0, 128)).astype(F32))
    pick_mate = hot(own_ids == row_of(sg, y_mate, slice(0, 128)).astype(F32))
    d_send[0:96, :] = mm(picked[128:224, 0:128], pick_mate).astype(BF)
    d_send[96:192, :] = mm(picked[128:224, 128:256], pick_mate).astype(BF)
    copy(d_send, d_recv, dy_s.at[0], dy_r.at[0], p, y_mate * 8 + e).start()
    d_re = mm(picked[0:96, 0:128], pick_own)
    d_im = mm(picked[0:96, 128:256], pick_own)

    a_row0 = column(row_of(sc, c, slice(0, 128)))
    a_row1 = column(twice(row_of(sc, c, slice(128, 192))))
    lane_at = jnp.where(lane < 64, lane, lane + 448.0) + (e * 64).astype(F32)
    fold = jnp.concatenate(
        [
            jnp.concatenate([hot(a_row0 == lane_at), hot(a_row0 == lane_at + 1024.0)], axis=1),
            jnp.concatenate([hot(a_row1 == lane_at), hot(a_row1 == lane_at + 1024.0)], axis=1)[0:64],
        ],
        axis=0,
    )
    for t in range(1, 4):
        y_from = (y + t) % 4
        arrived(t_recv.at[y_from], ty_r.at[y_from])
    for b in range(3):
        raw = jnp.concatenate([t_recv[i, b * 64 : b * 64 + 64, :] for i in range(4)], axis=0)
        part[b * 192 : b * 192 + 192, :] = mm(fold, raw).astype(BF)
    arrived(d_recv, dy_r.at[0])
    part[576:672, :] = (d_re + d_recv[0:96, :].astype(F32)).astype(BF)
    part[672:768, :] = (d_im + d_recv[96:192, :].astype(F32)).astype(BF)

    def piece(ref, i):
        return ref.at[pl.ds(pl.multiple_of(i * 96, 96), 96)]

    for t in range(1, 8):
        to = (e + t) % 8
        copy(piece(part, to), rs_recv.at[e], e3_s.at[t - 1], e3_r.at[e], p, base + to).start()
    c_relay(1)
    total = part[pl.ds(pl.multiple_of(e * 96, 96), 96), :].astype(F32)
    for t in range(1, 8):
        at = (e + t) % 8
        arrived(rs_recv.at[at], e3_r.at[at])
        total = total + rs_recv[at].astype(F32)
    full[pl.ds(pl.multiple_of(e * 96, 96), 96), :] = total.astype(BF)

    for t in range(1, 8):
        to = (e + t) % 8
        copy(piece(full, e), piece(full, e), e4_s.at[t - 1], e4_r.at[e], p, base + to).start()
    c_relay(2)
    g_relay(1)
    for t in range(1, 8):
        at = (e + t) % 8
        arrived(piece(full, at), e4_r.at[at])
    for b in range(3):
        acat[:, b * 128 : b * 128 + 128] = full[b * 192 : b * 192 + 192, :]

    g_re, g_im = right_side(fc_v[0], fc_v[1])
    a_now = acat[...]
    off_re = (-mm(a_now, g_re)).astype(BF)
    off_im = (-mm(a_now, g_im)).astype(BF)
    r_re, r_im = right_side(off_re, off_im)
    rhs[0, :, 0:128] = r_re
    rhs[0, :, 128:256] = r_im

    c_relay(3)
    c_finish()

    ft_r = mm(rl[0:128, :], ftc[...])
    lane384 = lax.broadcasted_iota(jnp.int32, (128, 384), 1)
    is_im = ((lane384 >= 128) & (lane384 < 256)) | (lane384 >= 320)
    f_re = jnp.where(is_im, -ft_r, ft_r).astype(BF)
    f_im = jnp.concatenate(
        [ft_r[:, 128:256], ft_r[:, 0:128], pltpu.roll(ft_r[:, 256:384], 64, 1)], axis=1
    ).astype(BF)
    a_low = acat[0:128, :]
    a_high = jnp.concatenate([acat[128:192, :], acat[128:192, :]], axis=0)
    off_t = jnp.concatenate(
        [
            -mm_nt(f_re, a_low),
            -mm_nt(f_im, a_low),
            -jnp.where(lane < 64, mm_nt(f_re, a_high), mm_nt(f_im, a_high)),
        ],
        axis=1,
    ).astype(BF)
    none = jnp.zeros((128, 128), BF)
    up0 = col0 - 2048.0
    up1 = col1 - 2048.0
    lane_hi = jnp.where(lane < 64, lane, lane - 64.0) + 128.0
    near0 = hot(up0 == lane)
    near1 = hot(up1 == lane)
    far0 = up0 == lane_hi
    far1 = up1 == lane_hi
    sub = iota((128, 128), 0)
    q0 = jnp.concatenate([near0, none, hot(far0 & (lane < 64))], axis=1)
    q1 = jnp.concatenate([none, near0, hot(far0 & (lane >= 64))], axis=1)
    q2 = jnp.concatenate(
        [
            jnp.where(sub < 64, near1.astype(F32), 0.0).astype(BF),
            jnp.where(sub >= 64, near1.astype(F32), 0.0).astype(BF),
            hot(far1 & ((lane < 64) == (sub < 64))),
        ],
        axis=1,
    )
    up_near = jnp.concatenate([near0, near1[0:64]], axis=0)
    up_far = jnp.concatenate([hot(far0), hot(far1)[0:64]], axis=0)[:, 0:64]
    a_rows = mm(up_near, acat[0:128, :]) + mm(up_far, acat[128:192, :])
    rows_all = a_rows + jnp.concatenate([off_t.astype(F32), jnp.zeros((64, 384), F32)], axis=0)
    q_all = jnp.concatenate([q0, q1, q2], axis=0)
    ag = mm_nt(rows_all.astype(BF), q_all)
    up_re = jnp.concatenate([q0, q2[0:64]], axis=0)
    up_im = jnp.concatenate([q1, q2[64:128]], axis=0)
    rest = jnp.zeros((32, 128), F32)
    tail = jnp.zeros((64, 128), F32)
    in_re = jnp.concatenate([full[576:672, :].astype(F32), rest], axis=0) - mm_nt(f_re, off_t)
    in_im = jnp.concatenate([full[672:768, :].astype(F32), rest], axis=0) - mm_nt(f_im, off_t)
    agcat[:, 0:128] = (
        ag[:, 0:128] + mm_nt(up_re, off_t) + jnp.concatenate([in_re, tail], axis=0)
    ).astype(BF)
    agcat[:, 128:256] = (
        ag[:, 128:256] + mm_nt(up_im, off_t) + jnp.concatenate([in_im, tail], axis=0)
    ).astype(BF)
    agcat[:, 256:384] = ag[:, 256:384].astype(BF)

    g_relay(2)

    gg_re, gg_im = right_side(fg_v[0], fg_v[1])
    ag_now = agcat[...]
    goff_re = (-mm(ag_now, gg_re)).astype(BF)
    goff_im = (-mm(ag_now, gg_im)).astype(BF)
    r_re, r_im = right_side(goff_re, goff_im)
    for h in range(2):
        rhs[1 + h, :, 0:128] = r_re[:, h * 128 : h * 128 + 128]
        rhs[1 + h, :, 128:256] = r_im[:, h * 128 : h * 128 + 128]

    w_im = pw[0, 0]
    w_re = pw[0, 1]

    def density(i, quarter, half):
        rows = pl.ds(pl.multiple_of(quarter * 512 + half * 256, 256), 256)
        ft = ftc[rows, :] if i == 0 else ftg[rows, :]
        rest_of = diag_v[i, rows, :].astype(F32) - mm(ft, rhs[i])
        rest_of = rest_of.astype(BF).astype(F32)
        return w_im * rest_of[:, 128:256] + w_re * rest_of[:, 0:128]

    x_next = (x + 1) % 4
    x_prev = (x + 3) % 4
    x_far = (x + 2) % 4
    p_next = x_next * 4 + zh
    p_prev = x_prev * 4 + zh

    def half_of(ref, h):
        return ref.at[pl.ds(h * 256, 256)]

    def opposite(i):
        for h, to in ((0, p_next), (1, p_prev)):
            s_opp[i, h] = density(i, x_far, h).astype(BF)
            copy(s_opp.at[i, h], r_opp.at[i, h], op_s.at[i, h], op_r.at[i, h], to, leaf).start()

    def neighbours(i):
        def send(side, h, to):
            n = side * 2 + h
            copy(half_of(s_nb.at[i, side], h), half_of(r_nb.at[i, side], h), nb_s.at[i, n], nb_r.at[i, n], to, leaf).start()

        s_nb[i, 0, 256:512, :] = density(i, x_next, 1).astype(BF)
        send(0, 1, p_next)
        s_nb[i, 1, 0:256, :] = density(i, x_prev, 0).astype(BF)
        send(1, 0, p_prev)
        mine = density(i, x_next, 0)
        arrived(r_opp.at[i, 0], op_r.at[i, 0])
        s_nb[i, 0, 0:256, :] = (mine + r_opp[i, 0].astype(F32)).astype(BF)
        send(0, 0, p_next)
        mine = density(i, x_prev, 1)
        arrived(r_opp.at[i, 1], op_r.at[i, 1])
        s_nb[i, 1, 256:512, :] = (mine + r_opp[i, 1].astype(F32)).astype(BF)
        send(1, 1, p_prev)

    def own_part(i):
        for h in range(2):
            own[i, h * 256 : h * 256 + 256, :] = density(i, x, h)

    def along_z(i):
        for n in (1, 2, 0, 3):
            arrived(half_of(r_nb.at[i, n // 2], n % 2), nb_r.at[i, n])

        def summed(to):
            rows = pl.ds(pl.multiple_of(to * 128, 128), 128)
            return own[i, rows, :] + r_nb[i, 0, rows, :].astype(F32) + r_nb[i, 1, rows, :].astype(F32)

        for t in (2, 1, 3):
            to = (zh + t) % 4
            sz[i, to] = summed(to).astype(BF)
            copy(sz.at[i, to], rz.at[i, zh], z_s.at[i, t - 1], z_r.at[i, zh], x * 4 + to, leaf).start()
        keep[i] = summed(zh)

    def result(i):
        total = keep[i]
        for t in (1, 3, 2):
            z_from = (zh + t) % 4
            arrived(rz.at[i, z_from], z_r.at[i, z_from])
            total = total + rz[i, z_from].astype(F32)
        return total

    opposite(0)
    neighbours(0)
    own_part(0)

    g_relay(3)
    g_finish()
    for i in (6, 7, 11, 12):
        loads[i].wait()
    opposite(1)
    opposite(2)
    along_z(0)
    neighbours(1)
    neighbours(2)
    own_part(1)
    along_z(1)
    own_part(2)
    along_z(2)
    out_c[...] = result(0)
    out_g[:, 0:128] = result(1)
    out_g[:, 128:256] = result(2)

    for t in range(3):
        sent(t_send.at[0], ty_s.at[t])
        for i in range(3):
            sent(sz.at[0, 0], z_s.at[i, t])
    for i in range(3):
        for h in range(2):
            sent(s_opp.at[0, 0], op_s.at[i, h])
        for n in range(4):
            sent(s_opp.at[0, 0], nb_s.at[i, n])
    sent(d_send, dy_s.at[0])
    for t in range(7):
        sent(piece(part, 0), e3_s.at[t])
        sent(piece(full, 0), e4_s.at[t])
    for j in range(4):

        @pl.when((zl < 3) & (j <= zl))
        def _(j=j):
            sent(c_block(0, 0, 0), cz_s.at[j])
            sent(g_block(0, 0), gz_s.at[j])

        @pl.when((zl > 0) & (j >= zl))
        def _(j=j):
            sent(c_block(0, 0, 0), cz_s.at[4 + j])
            sent(g_block(0, 0), gz_s.at[4 + j])

        sent(c_block(0, 0, 0), cy_s.at[j])
        sent(c_block(0, 0, 0), cc_s.at[j])
        sent(c_block(0, 0, 0), cc_s.at[4 + j])
        sent(g_block(0, 0), gc_s.at[j])


def local(*args):
    vm = pltpu.VMEM
    dma = pltpu.SemaphoreType.DMA
    scratch = [
        vm((2, 192), jnp.int32),
        vm((4, 192), jnp.int32),
        pltpu.SMEM((1, 2), F32),
        vm((128, 2048), BF),
        vm((2, 192, 128), BF),
        vm((2, 192, 256), BF),
        vm((3, 2048, 256), BF),
        vm((2048, 384), BF),
        vm((2048, 384), BF),
        vm((2048, 512), BF),
        vm((256, 2048), BF),
        vm((2, 192, 128), BF),
        vm((4, 192, 128), BF),
        vm((192, 128), BF),
        vm((192, 128), BF),
        vm((768, 128), BF),
        vm((8, 96, 128), BF),
        vm((768, 128), BF),
        vm((192, 384), BF),
        vm((192, 384), BF),
        vm((3, 384, 256), BF),
        vm((3, 2, 256, 128), BF),
        vm((3, 2, 256, 128), BF),
        vm((3, 2, 512, 128), BF),
        vm((3, 2, 512, 128), BF),
        vm((3, 512, 128), F32),
        vm((3, 4, 128, 128), BF),
        vm((3, 4, 128, 128), BF),
        vm((3, 128, 128), F32),
        dma((13,)),
        dma((3,)),
        dma((4,)),
        dma((1,)),
        dma((1,)),
        dma((7,)),
        dma((8,)),
        dma((7,)),
        dma((8,)),
        dma((8,)),
        dma((4,)),
        dma((4,)),
        dma((4,)),
        dma((8,)),
        dma((8,)),
        dma((8,)),
        dma((4,)),
        dma((4,)),
        dma((4,)),
        dma((3, 2)),
        dma((3, 2)),
        dma((3, 4)),
        dma((3, 4)),
        dma((3, 3)),
        dma((3, 4)),
    ]
    hbm = pl.BlockSpec(memory_space=pltpu.HBM)
    vm_spec = pl.BlockSpec(memory_space=pltpu.VMEM)
    return pl.pallas_call(
        kernel,
        out_shape=[
            jax.ShapeDtypeStruct((128, 128), F32),
            jax.ShapeDtypeStruct((128, 256), F32),
        ],
        in_specs=[hbm] * 8,
        out_specs=[vm_spec, vm_spec],
        scratch_shapes=scratch,
        compiler_params=pltpu.CompilerParams(
            collective_id=0, has_side_effects=True, vmem_limit_bytes=60 * 1024 * 1024
        ),
        cost_estimate=pl.CostEstimate(flops=3_000_000_000, bytes_accessed=5_000_000, transcendentals=0),
    )(*args)


def solution(mesh):
    placed = (
        P("pole", None, "leaf", None),
        P("pole", None, None, "leaf"),
        P("pole", None, None, "leaf"),
        P("pole", None, None, "leaf"),
        P("pole", None, None, "leaf"),
        P(),
        P(),
        P("pole", None),
    )
    return jax.shard_map(
        local,
        mesh=mesh,
        in_specs=placed,
        out_specs=(P("pole", "leaf"), P("pole", "leaf")),
        check_vma=False,
    )
```

```python
import jax
import jax.numpy as jnp
from jax import lax
from jax.experimental import pallas as pl
from jax.experimental.pallas import tpu as pltpu
from jax.sharding import PartitionSpec as P

MESH = pl.DeviceIdType.MESH
BF = jnp.bfloat16
F32 = jnp.float32


def mm(a, b):
    return jnp.dot(a, b, preferred_element_type=F32)


def mm_nt(a, b):
    return lax.dot_general(a, b, (((1,), (1,)), ((), ())), preferred_element_type=F32)


def hot(cond):
    return jnp.where(cond, 1.0, 0.0).astype(BF)


def column(row):
    return jnp.transpose(jnp.broadcast_to(row.astype(F32), (128, 128)))


def iota(shape, dim):
    return lax.broadcasted_iota(jnp.int32, shape, dim).astype(F32)


def twice(row):
    return jnp.concatenate([row, row], axis=1)


def row_of(ref, index, lanes):
    row = ref[0:1, lanes]
    for i in range(1, ref.shape[0]):
        row = jnp.where(index == i, ref[i : i + 1, lanes], row)
    return row


def right_side(off_re, off_im):
    re_col = jnp.concatenate([off_re[:128], -off_im[:128], off_re[128:], -off_im[128:]], axis=0)
    im_col = jnp.concatenate([off_im[:128], off_re[:128], off_im[128:], off_re[128:]], axis=0)
    return re_col, im_col


def transposed(ref, cols):
    parts = [
        ref[0, 0:128, cols],
        ref[1, 0:128, cols],
        jnp.concatenate([ref[0, 128:192, cols], ref[1, 128:192, cols]], axis=0),
    ]
    return jnp.concatenate([jnp.transpose(p.astype(F32)) for p in parts], axis=1).astype(BF)


def kernel(
    root,
    fc,
    fg,
    dc,
    dg,
    sc_hbm,
    sg_hbm,
    pw_hbm,
    out_c,
    out_g,
    sc,
    sg,
    pw,
    root_v,
    fc_v,
    fg_v,
    diag_v,
    ftc,
    ftg,
    oh,
    rl,
    t_send,
    t_recv,
    d_send,
    d_recv,
    part,
    sw_recv,
    half,
    rs_recv,
    full,
    acat,
    agcat,
    rhs,
    s_out,
    r_opp,
    r_nb,
    dens,
    sz,
    rz,
    keep,
    lsem,
    ty_s,
    ty_r,
    dy_s,
    dy_r,
    sw_s,
    sw_r,
    e3_s,
    e3_r,
    e4_s,
    e4_r,
    e5_s,
    e5_r,
    cz_s,
    cz_r,
    cy_s,
    cy_r,
    cc_s,
    cc_r,
    gz_s,
    gz_r,
    gc_s,
    gc_r,
    op_s,
    op_r,
    nb_s,
    nb_r,
    z_s,
    z_r,
    across,
):
    p = lax.axis_index("pole")
    leaf = lax.axis_index("leaf")
    x = p // 4
    zh = p % 4
    y = leaf // 8
    e = leaf % 8
    zl = e // 2
    k = e % 2
    c = y // 2
    yp = y % 2
    y_mate = y + 1 - 2 * yp
    base = y * 8

    def copy(src, dst, ssem, rsem, pole_to, leaf_to):
        return pltpu.make_async_remote_copy(
            src_ref=src,
            dst_ref=dst,
            send_sem=ssem,
            recv_sem=rsem,
            device_id=(pole_to, leaf_to),
            device_id_type=MESH,
        )

    def arrived(dst, rsem):
        copy(dst, dst, rsem, rsem, p, leaf).wait_recv()

    def sent(src, ssem):
        copy(src, src, ssem, ssem, p, leaf).wait_send()

    barrier = pltpu.get_barrier_semaphore()

    def greet(pole_to, leaf_to):
        pl.semaphore_signal(barrier, inc=1, device_id=(pole_to, leaf_to), device_id_type=MESH)

    mate = base + e + 1 - 2 * k
    for t in (1, 3):
        greet(x * 4 + (zh + t) % 4, leaf)
    for t in (2, 1, 3):
        greet(p, (y + t) % 4 * 8 + e)
    for t in range(1, 4):
        greet(p, base + (e + 2 * t) % 8)
    greet((x + 1) % 4 * 4 + zh, leaf)
    greet((x + 3) % 4 * 4 + zh, leaf)
    greet(p, mate)

    loads = [
        pltpu.make_async_copy(root.at[0, 0], root_v.at[0:64], lsem.at[0]),
        pltpu.make_async_copy(root.at[0, 1], root_v.at[64:128], lsem.at[1]),
        pltpu.make_async_copy(fc.at[0], fc_v, lsem.at[2]),
        pltpu.make_async_copy(fg.at[0], fg_v, lsem.at[3]),
        pltpu.make_async_copy(dc.at[0, 0], diag_v.at[0, :, 0:128], lsem.at[4]),
        pltpu.make_async_copy(dc.at[0, 1], diag_v.at[0, :, 128:256], lsem.at[5]),
        pltpu.make_async_copy(dg.at[0, 0, :, 0:128], diag_v.at[1, :, 0:128], lsem.at[6]),
        pltpu.make_async_copy(dg.at[0, 1, :, 0:128], diag_v.at[1, :, 128:256], lsem.at[7]),
        pltpu.make_async_copy(sc_hbm, sc, lsem.at[8]),
        pltpu.make_async_copy(sg_hbm, sg, lsem.at[9]),
        pltpu.make_async_copy(pw_hbm, pw, lsem.at[10]),
        pltpu.make_async_copy(dg.at[0, 0, :, 128:256], diag_v.at[2, :, 0:128], lsem.at[11]),
        pltpu.make_async_copy(dg.at[0, 1, :, 128:256], diag_v.at[2, :, 128:256], lsem.at[12]),
    ]
    for i in (8, 9, 2, 3, 0, 1, 4, 5, 10, 6, 7, 11, 12):
        loads[i].start()

    own_c = pl.multiple_of((yp * 8 + e) * 128, 128)
    own_g = pl.multiple_of(e * 256, 256)
    loads[2].wait()
    ftc[pl.ds(own_c, 128), :] = transposed(fc_v, slice(0, 128))
    loads[3].wait()
    ftg[pl.ds(own_g, 128), :] = transposed(fg_v, slice(0, 128))
    ftg[pl.ds(pl.multiple_of(own_g + 128, 128), 128), :] = transposed(fg_v, slice(128, 256))

    loads[8].wait()
    loads[9].wait()
    loads[10].wait()
    child_rows = [sc[0:1, 0:128], twice(sc[0:1, 128:192]), sc[1:2, 0:128], twice(sc[1:2, 128:192])]
    hot_rows = jnp.concatenate(child_rows, axis=1).astype(F32)

    def build_hot(i, carry):
        at = pl.multiple_of(i * 128, 128)
        ids = iota((128, 512), 0) + (i * 128).astype(F32)
        oh[pl.ds(at, 128), :] = hot(ids == hot_rows)
        return carry

    lax.fori_loop(0, 16, build_hot, 0)
    loads[0].wait()
    loads[1].wait()
    taken = mm(root_v[...], oh[...])
    low_lanes = iota((64, 128), 1) < 64
    for ch in range(2):
        at = ch * 256
        t_send[ch, 0:64, :] = taken[0:64, at : at + 128].astype(BF)
        t_send[ch, 64:128, :] = taken[64:128, at : at + 128].astype(BF)
        t_send[ch, 128:192, :] = jnp.where(
            low_lanes, taken[0:64, at + 128 : at + 256], taken[64:128, at + 128 : at + 256]
        ).astype(BF)

    pl.semaphore_wait(barrier, 11)
    for t in (1, 3):
        pl.semaphore_signal(
            across, inc=1, device_id=(x * 4 + (zh + t) % 4, leaf), device_id_type=MESH
        )

    for t in range(1, 4):
        y_to = (y + t) % 4
        copy(t_send.at[y_to // 2], t_recv.at[y], ty_s.at[t - 1], ty_r.at[y], p, y_to * 8 + e).start()
    t_recv[pl.ds(y, 1)] = t_send[pl.ds(c, 1)]

    def c_block(yy, j, kk):
        return ftc.at[pl.ds(pl.multiple_of((yy * 8 + j * 2 + kk) * 128, 128), 128)]

    def g_block(j, kk, part_at):
        return ftg.at[pl.ds(pl.multiple_of((j * 2 + kk) * 256 + part_at * 128, 128), 128)]

    def c_up(j):
        return copy(c_block(yp, j, k), c_block(yp, j, k), cz_s.at[j], cz_r.at[j], p, base + e + 2)

    def c_down(j):
        return copy(c_block(yp, j, k), c_block(yp, j, k), cz_s.at[4 + j], cz_r.at[j], p, base + e - 2)

    def c_side(j):
        return copy(c_block(yp, j, k), c_block(yp, j, k), cy_s.at[j], cy_r.at[j], p, y_mate * 8 + e)

    def c_core(yy, j):
        i = yy * 4 + j
        return copy(c_block(yy, j, k), c_block(yy, j, k), cc_s.at[i], cc_r.at[i], p, base + e + 1 - 2 * k)

    def g_up(j, b):
        return copy(g_block(j, k, b), g_block(j, k, b), gz_s.at[0, b, j], gz_r.at[b, j], p, base + e + 2)

    def g_down(j, b):
        return copy(g_block(j, k, b), g_block(j, k, b), gz_s.at[1, b, j], gz_r.at[b, j], p, base + e - 2)

    def g_core(j, b):
        return copy(g_block(j, k, b), g_block(j, k, b), gc_s.at[b, j], gc_r.at[b, j], p, mate)

    def c_first():
        @pl.when(zl < 3)
        def _():
            c_up(zl).start()

        @pl.when(zl > 0)
        def _():
            c_down(zl).start()

        c_core(yp, zl).start()

    def g_first(b):
        @pl.when(zl < 3)
        def _():
            g_up(zl, b).start()

        @pl.when(zl > 0)
        def _():
            g_down(zl, b).start()

        g_core(zl, b).start()

    def c_relay(s):
        @pl.when(zl >= s)
        def _():
            j = zl - s
            arrived(c_block(yp, j, k), cz_r.at[j])

            @pl.when(zl < 3)
            def _():
                c_up(j).start()

            c_side(j).start()
            c_core(yp, j).start()

        @pl.when(zl + s <= 3)
        def _():
            j = zl + s
            arrived(c_block(yp, j, k), cz_r.at[j])

            @pl.when(zl > 0)
            def _():
                c_down(j).start()

            c_side(j).start()
            c_core(yp, j).start()

    def g_relay(s, b):
        @pl.when(zl >= s)
        def _():
            j = zl - s
            arrived(g_block(j, k, b), gz_r.at[b, j])

            @pl.when(zl < 3)
            def _():
                g_up(j, b).start()

            g_core(j, b).start()

        @pl.when(zl + s <= 3)
        def _():
            j = zl + s
            arrived(g_block(j, k, b), gz_r.at[b, j])

            @pl.when(zl > 0)
            def _():
                g_down(j, b).start()

            g_core(j, b).start()

    def c_finish():
        for i in range(4):
            arrived(c_block(1 - yp, i, k), cy_r.at[i])
            c_core(1 - yp, i).start()
        for i in range(8):
            arrived(c_block(i // 4, i % 4, 1 - k), cc_r.at[i])

    c_first()
    g_first(0)
    g_first(1)

    col0 = column(row_of(sg, y, slice(0, 128)))
    col1 = column(twice(row_of(sg, y, slice(128, 192))))
    col_mate = column(row_of(sg, y_mate, slice(0, 128)))
    lane = iota((128, 128), 1)

    def build_low(i, carry):
        at = pl.multiple_of(i * 128, 128)
        ids = lane + (i * 128).astype(F32)
        rl[0:128, pl.ds(at, 128)] = hot(col0 == ids)
        rl[128:256, pl.ds(at, 128)] = hot(col_mate == ids)
        return carry

    lax.fori_loop(0, 16, build_low, 0)
    loads[4].wait()
    loads[5].wait()
    picked = mm(rl[...], diag_v[0]).astype(BF)
    own_ids = iota((128, 128), 0) + own_c.astype(F32)
    pick_own = hot(own_ids == row_of(sg, y, slice(0, 128)).astype(F32))
    pick_mate = hot(own_ids == row_of(sg, y_mate, slice(0, 128)).astype(F32))
    d_send[0:96, :] = mm(picked[128:224, 0:128], pick_mate).astype(BF)
    d_send[96:192, :] = mm(picked[128:224, 128:256], pick_mate).astype(BF)
    copy(d_send, d_recv, dy_s.at[0], dy_r.at[0], p, y_mate * 8 + e).start()
    d_re = mm(picked[0:96, 0:128], pick_own)
    d_im = mm(picked[0:96, 128:256], pick_own)

    a_row0 = column(row_of(sc, c, slice(0, 128)))
    a_row1 = column(twice(row_of(sc, c, slice(128, 192))))
    lane_at = jnp.where(lane < 64, lane, lane + 448.0) + (e * 64).astype(F32)
    fold = jnp.concatenate(
        [
            jnp.concatenate([hot(a_row0 == lane_at), hot(a_row0 == lane_at + 1024.0)], axis=1),
            jnp.concatenate([hot(a_row1 == lane_at), hot(a_row1 == lane_at + 1024.0)], axis=1)[0:64],
        ],
        axis=0,
    )
    c_relay(1)
    for t in range(1, 4):
        y_from = (y + t) % 4
        arrived(t_recv.at[y_from], ty_r.at[y_from])
    for b in range(3):
        raw = jnp.concatenate([t_recv[i, b * 64 : b * 64 + 64, :] for i in range(4)], axis=0)
        part[b * 192 : b * 192 + 192, :] = mm(fold, raw).astype(BF)
    arrived(d_recv, dy_r.at[0])
    part[576:672, :] = (d_re + d_recv[0:96, :].astype(F32)).astype(BF)
    part[672:768, :] = (d_im + d_recv[96:192, :].astype(F32)).astype(BF)

    c_side(zl).start()

    def piece(ref, i):
        return ref.at[pl.ds(pl.multiple_of(i * 96, 96), 96)]

    def side_rows(kk):
        return pl.ds(pl.multiple_of(kk * 384, 128), 384)

    swap = copy(part.at[side_rows(1 - k)], sw_recv, sw_s.at[0], sw_r.at[0], p, mate)
    swap.start()
    arrived(sw_recv, sw_r.at[0])
    half[...] = (part[side_rows(k), :].astype(F32) + sw_recv[...].astype(F32)).astype(BF)

    for t in (2, 1, 3):
        to = (zl + t) % 4
        copy(piece(half, to), rs_recv.at[zl], e3_s.at[t - 1], e3_r.at[zl], p, base + to * 2 + k).start()
    c_relay(2)
    total = half[pl.ds(pl.multiple_of(zl * 96, 96), 96), :].astype(F32)
    for t in (1, 3, 2):
        at = (zl + t) % 4
        arrived(rs_recv.at[at], e3_r.at[at])
        total = total + rs_recv[at].astype(F32)
    mine = k * 4 + zl
    full[pl.ds(pl.multiple_of(mine * 96, 96), 96), :] = total.astype(BF)

    for t in (2, 1, 3):
        to = (zl + t) % 4
        copy(piece(full, mine), piece(full, mine), e4_s.at[t - 1], e4_r.at[zl], p, base + to * 2 + k).start()

    def to_mate(at):
        i = k * 4 + at
        copy(piece(full, i), piece(full, i), e5_s.at[at], e5_r.at[at], p, mate).start()

    to_mate(zl)
    c_relay(3)
    for t in (1, 3, 2):
        at = (zl + t) % 4
        arrived(piece(full, k * 4 + at), e4_r.at[at])
        to_mate(at)
    for at in range(4):
        arrived(piece(full, (1 - k) * 4 + at), e5_r.at[at])
    for b in range(3):
        acat[:, b * 128 : b * 128 + 128] = full[b * 192 : b * 192 + 192, :]

    g_relay(1, 0)
    g_relay(1, 1)
    g_re, g_im = right_side(fc_v[0], fc_v[1])
    a_now = acat[...]
    off_re = (-mm(a_now, g_re)).astype(BF)
    off_im = (-mm(a_now, g_im)).astype(BF)
    r_re, r_im = right_side(off_re, off_im)
    rhs[0, :, 0:128] = r_re
    rhs[0, :, 128:256] = r_im

    c_finish()

    w_im = pw[0, 0]
    w_re = pw[0, 1]
    x_next = (x + 1) % 4
    x_prev = (x + 3) % 4
    p_next = x_next * 4 + zh
    p_prev = x_prev * 4 + zh

    def process(i, quarter, role, b):
        at = b * 128
        ft_ref = ftc if i == 0 else ftg
        rows = [pl.ds(pl.multiple_of(quarter * 512 + h * 256 + at, 128), 128) for h in range(2)]
        ft = jnp.concatenate([ft_ref[r, :] for r in rows], axis=0)
        reduced = mm(ft, rhs[i])
        here = pl.ds(at, 128)
        for h in range(2):
            inverse = diag_v[i, rows[h], :].astype(F32) - reduced[h * 128 : h * 128 + 128]
            inverse = inverse.astype(BF).astype(F32)
            value = w_im * inverse[:, 128:256] + w_re * inverse[:, 0:128]
            dens[i, role, h, here] = value
            s_out[i, role, h, here] = value.astype(BF)

        @pl.when(role == 2)
        def _():
            opp_copy(i, 0, b, p_next).start()
            opp_copy(i, 1, b, p_prev).start()

        @pl.when(role == 1)
        def _():
            nb_copy(i, 0, 1, b).start()

        @pl.when(role == 3)
        def _():
            nb_copy(i, 1, 0, b).start()

    def opp_copy(i, h, b, to):
        here = pl.ds(b * 128, 128)
        return copy(s_out.at[i, 2, h, here], r_opp.at[i, h, here], op_s.at[i, h, b], op_r.at[i, h, b], to, leaf)

    def nb_copy(i, side, h, b):
        here = pl.ds(b * 128, 128)
        return copy(
            s_out.at[i, 1 + 2 * side, h, here],
            r_nb.at[i, side, h, here],
            nb_s.at[i, side, h, b],
            nb_r.at[i, side, h, b],
            p_prev if side else p_next,
            leaf,
        )

    def complete(i, b):
        here = pl.ds(b * 128, 128)
        for side in range(2):
            arrived(r_opp.at[i, side, here], op_r.at[i, side, b])
            s_out[i, 1 + 2 * side, side, here] = (
                dens[i, 1 + 2 * side, side, here] + r_opp[i, side, here].astype(F32)
            ).astype(BF)
            nb_copy(i, side, side, b).start()

    def z_copy(i, to):
        return copy(sz.at[i, to], rz.at[i, zh], z_s.at[i, to], z_r.at[i, zh], x * 4 + to, leaf)

    def along_z(i, b):
        here = pl.ds(b * 128, 128)
        for h in range(2):
            for side in range(2):
                arrived(r_nb.at[i, side, h, here], nb_r.at[i, side, h, b])
        for h in range(2):
            to = 2 * h + b
            total = dens[i, 0, h, here] + r_nb[i, 0, h, here].astype(F32) + r_nb[i, 1, h, here].astype(F32)

            @pl.when(zh != to)
            def _():
                sz[i, to] = total.astype(BF)
                z_copy(i, to).start()

            @pl.when(zh == to)
            def _():
                keep[i] = total

    def result(i):
        total = keep[i]
        for t in (1, 3, 2):
            z_from = (zh + t) % 4
            arrived(rz.at[i, z_from], z_r.at[i, z_from])
            total = total + rz[i, z_from].astype(F32)
        return total

    for b in range(2):
        for r in (2, 1, 3, 0):
            process(0, (x + r) % 4, r, b)

    ft_r = mm(rl[0:128, :], ftc[...])
    lane384 = lax.broadcasted_iota(jnp.int32, (128, 384), 1)
    is_im = ((lane384 >= 128) & (lane384 < 256)) | (lane384 >= 320)
    f_re = jnp.where(is_im, -ft_r, ft_r).astype(BF)
    f_im = jnp.concatenate(
        [ft_r[:, 128:256], ft_r[:, 0:128], pltpu.roll(ft_r[:, 256:384], 64, 1)], axis=1
    ).astype(BF)
    a_low = acat[0:128, :]
    a_high = jnp.concatenate([acat[128:192, :], acat[128:192, :]], axis=0)
    off_t = jnp.concatenate(
        [
            -mm_nt(f_re, a_low),
            -mm_nt(f_im, a_low),
            -jnp.where(lane < 64, mm_nt(f_re, a_high), mm_nt(f_im, a_high)),
        ],
        axis=1,
    ).astype(BF)
    none = jnp.zeros((128, 128), BF)
    up0 = col0 - 2048.0
    up1 = col1 - 2048.0
    lane_hi = jnp.where(lane < 64, lane, lane - 64.0) + 128.0
    near0 = hot(up0 == lane)
    near1 = hot(up1 == lane)
    far0 = up0 == lane_hi
    far1 = up1 == lane_hi
    sub = iota((128, 128), 0)
    q0 = jnp.concatenate([near0, none, hot(far0 & (lane < 64))], axis=1)
    q1 = jnp.concatenate([none, near0, hot(far0 & (lane >= 64))], axis=1)
    q2 = jnp.concatenate(
        [
            jnp.where(sub < 64, near1.astype(F32), 0.0).astype(BF),
            jnp.where(sub >= 64, near1.astype(F32), 0.0).astype(BF),
            hot(far1 & ((lane < 64) == (sub < 64))),
        ],
        axis=1,
    )
    up_near = jnp.concatenate([near0, near1[0:64]], axis=0)
    up_far = jnp.concatenate([hot(far0), hot(far1)[0:64]], axis=0)[:, 0:64]
    a_rows = mm(up_near, acat[0:128, :]) + mm(up_far, acat[128:192, :])
    rows_all = a_rows + jnp.concatenate([off_t.astype(F32), jnp.zeros((64, 384), F32)], axis=0)
    q_all = jnp.concatenate([q0, q1, q2], axis=0)
    ag = mm_nt(rows_all.astype(BF), q_all)
    up_re = jnp.concatenate([q0, q2[0:64]], axis=0)
    up_im = jnp.concatenate([q1, q2[64:128]], axis=0)
    rest = jnp.zeros((32, 128), F32)
    tail = jnp.zeros((64, 128), F32)
    in_re = jnp.concatenate([full[576:672, :].astype(F32), rest], axis=0) - mm_nt(f_re, off_t)
    in_im = jnp.concatenate([full[672:768, :].astype(F32), rest], axis=0) - mm_nt(f_im, off_t)
    agcat[:, 0:128] = (
        ag[:, 0:128] + mm_nt(up_re, off_t) + jnp.concatenate([in_re, tail], axis=0)
    ).astype(BF)
    agcat[:, 128:256] = (
        ag[:, 128:256] + mm_nt(up_im, off_t) + jnp.concatenate([in_im, tail], axis=0)
    ).astype(BF)
    agcat[:, 256:384] = ag[:, 256:384].astype(BF)


    g_relay(2, 0)
    g_relay(2, 1)
    gg_re, gg_im = right_side(fg_v[0], fg_v[1])
    ag_now = agcat[...]
    goff_re = (-mm(ag_now, gg_re)).astype(BF)
    goff_im = (-mm(ag_now, gg_im)).astype(BF)
    r_re, r_im = right_side(goff_re, goff_im)
    for h in range(2):
        rhs[1 + h, :, 0:128] = r_re[:, h * 128 : h * 128 + 128]
        rhs[1 + h, :, 128:256] = r_im[:, h * 128 : h * 128 + 128]

    def g_quarter(q, b):
        arrived(g_block(q, 1 - k, b), gc_r.at[b, q])
        role = (q - x + 4) % 4
        process(1, q, role, b)
        process(2, q, role, b)

    for i in (6, 7, 11, 12):
        loads[i].wait()
    pl.semaphore_wait(across, 2)
    far = 3 * (1 - zl // 2)
    for b in range(2):
        g_quarter(zl, b)
    for b in range(2):
        complete(0, b)
    for b in range(2):
        g_quarter(zl + 1 - 2 * (zl // 2), b)
    for b in range(2):
        g_quarter((3 * zl + 2) % 5, b)
    for b in range(2):
        along_z(0, b)
    for b in range(2):
        g_relay(3, b)
        g_quarter(far, b)
    for b in range(2):
        for i in (1, 2):
            complete(i, b)
    for b in range(2):
        for i in (1, 2):
            along_z(i, b)
    out_c[...] = result(0)
    out_g[:, 0:128] = result(1)
    out_g[:, 128:256] = result(2)

    for t in range(3):
        sent(t_send.at[0], ty_s.at[t])
    for i in range(3):
        for to in range(4):

            @pl.when(zh != to)
            def _(i=i, to=to):
                sent(sz.at[0, 0], z_s.at[i, to])

        for b in range(2):
            for h in range(2):
                sent(sz.at[0, 0], op_s.at[i, h, b])
                for side in range(2):
                    sent(sz.at[0, 0], nb_s.at[i, side, h, b])
    sent(d_send, dy_s.at[0])
    sent(sw_recv, sw_s.at[0])
    for t in range(3):
        sent(piece(half, 0), e3_s.at[t])
        sent(piece(full, 0), e4_s.at[t])
    for t in range(4):
        sent(piece(full, 0), e5_s.at[t])
    for j in range(4):

        @pl.when((zl < 3) & (j <= zl))
        def _(j=j):
            sent(c_block(0, 0, 0), cz_s.at[j])
            for b in range(2):
                sent(g_block(0, 0, 0), gz_s.at[0, b, j])

        @pl.when((zl > 0) & (j >= zl))
        def _(j=j):
            sent(c_block(0, 0, 0), cz_s.at[4 + j])
            for b in range(2):
                sent(g_block(0, 0, 0), gz_s.at[1, b, j])

        sent(c_block(0, 0, 0), cy_s.at[j])
        sent(c_block(0, 0, 0), cc_s.at[j])
        sent(c_block(0, 0, 0), cc_s.at[4 + j])
        for b in range(2):
            sent(g_block(0, 0, 0), gc_s.at[b, j])


def local(*args):
    vm = pltpu.VMEM
    dma = pltpu.SemaphoreType.DMA
    scratch = [
        vm((2, 192), jnp.int32),
        vm((4, 192), jnp.int32),
        pltpu.SMEM((1, 2), F32),
        vm((128, 2048), BF),
        vm((2, 192, 128), BF),
        vm((2, 192, 256), BF),
        vm((3, 2048, 256), BF),
        vm((2048, 384), BF),
        vm((2048, 384), BF),
        vm((2048, 512), BF),
        vm((256, 2048), BF),
        vm((2, 192, 128), BF),
        vm((4, 192, 128), BF),
        vm((192, 128), BF),
        vm((192, 128), BF),
        vm((768, 128), BF),
        vm((384, 128), BF),
        vm((384, 128), BF),
        vm((4, 96, 128), BF),
        vm((768, 128), BF),
        vm((192, 384), BF),
        vm((192, 384), BF),
        vm((3, 384, 256), BF),
        vm((3, 4, 2, 256, 128), BF),
        vm((3, 2, 256, 128), BF),
        vm((3, 2, 2, 256, 128), BF),
        vm((3, 4, 2, 256, 128), F32),
        vm((3, 4, 128, 128), BF),
        vm((3, 4, 128, 128), BF),
        vm((3, 128, 128), F32),
        dma((13,)),
        dma((3,)),
        dma((4,)),
        dma((1,)),
        dma((1,)),
        dma((1,)),
        dma((1,)),
        dma((3,)),
        dma((4,)),
        dma((3,)),
        dma((4,)),
        dma((4,)),
        dma((4,)),
        dma((8,)),
        dma((4,)),
        dma((4,)),
        dma((4,)),
        dma((8,)),
        dma((8,)),
        dma((2, 2, 4)),
        dma((2, 4)),
        dma((2, 4)),
        dma((2, 4)),
        dma((3, 2, 2)),
        dma((3, 2, 2)),
        dma((3, 2, 2, 2)),
        dma((3, 2, 2, 2)),
        dma((3, 4)),
        dma((3, 4)),
        pltpu.SemaphoreType.REGULAR,
    ]
    hbm = pl.BlockSpec(memory_space=pltpu.HBM)
    vm_spec = pl.BlockSpec(memory_space=pltpu.VMEM)
    return pl.pallas_call(
        kernel,
        out_shape=[
            jax.ShapeDtypeStruct((128, 128), F32),
            jax.ShapeDtypeStruct((128, 256), F32),
        ],
        in_specs=[hbm] * 8,
        out_specs=[vm_spec, vm_spec],
        scratch_shapes=scratch,
        compiler_params=pltpu.CompilerParams(
            collective_id=0, has_side_effects=True, vmem_limit_bytes=60 * 1024 * 1024
        ),
        cost_estimate=pl.CostEstimate(flops=3_000_000_000, bytes_accessed=5_000_000, transcendentals=0),
    )(*args)


def solution(mesh):
    placed = (
        P("pole", None, "leaf", None),
        P("pole", None, None, "leaf"),
        P("pole", None, None, "leaf"),
        P("pole", None, None, "leaf"),
        P("pole", None, None, "leaf"),
        P(),
        P(),
        P("pole", None),
    )
    return jax.shard_map(
        local,
        mesh=mesh,
        in_specs=placed,
        out_specs=(P("pole", "leaf"), P("pole", "leaf")),
        check_vma=False,
    )
```

```python
import jax
import jax.numpy as jnp
from jax import lax
from jax.experimental import pallas as pl
from jax.experimental.pallas import tpu as pltpu
from jax.sharding import PartitionSpec as P

MESH = pl.DeviceIdType.MESH
BF = jnp.bfloat16
F32 = jnp.float32


def mm(a, b):
    return jnp.dot(a, b, preferred_element_type=F32)


def mm_nt(a, b):
    return lax.dot_general(a, b, (((1,), (1,)), ((), ())), preferred_element_type=F32)


def hot(cond):
    return jnp.where(cond, 1.0, 0.0).astype(BF)


def column(row):
    return jnp.transpose(jnp.broadcast_to(row.astype(F32), (128, 128)))


def iota(shape, dim):
    return lax.broadcasted_iota(jnp.int32, shape, dim).astype(F32)


def twice(row):
    return jnp.concatenate([row, row], axis=1)


def row_of(ref, index, lanes):
    row = ref[0:1, lanes]
    for i in range(1, ref.shape[0]):
        row = jnp.where(index == i, ref[i : i + 1, lanes], row)
    return row


def right_side(off_re, off_im):
    re_col = jnp.concatenate([off_re[:128], -off_im[:128], off_re[128:], -off_im[128:]], axis=0)
    im_col = jnp.concatenate([off_im[:128], off_re[:128], off_im[128:], off_re[128:]], axis=0)
    return re_col, im_col


def transposed(ref, cols):
    parts = [
        ref[0, 0:128, cols],
        ref[1, 0:128, cols],
        jnp.concatenate([ref[0, 128:192, cols], ref[1, 128:192, cols]], axis=0),
    ]
    return jnp.concatenate([jnp.transpose(p.astype(F32)) for p in parts], axis=1).astype(BF)


def kernel(
    root,
    fc,
    fg,
    dc,
    dg,
    sc_hbm,
    sg_hbm,
    pw_hbm,
    out_c,
    out_g,
    sc,
    sg,
    pw,
    root_v,
    fc_v,
    fg_v,
    diag_v,
    ftc,
    ftg,
    oh,
    rl,
    t_send,
    t_recv,
    d_send,
    d_recv,
    part,
    sw_recv,
    half,
    rs_recv,
    full,
    acat,
    agcat,
    rhs,
    s_out,
    r_opp,
    r_nb,
    dens,
    sz,
    rz,
    keep,
    lsem,
    ty_s,
    ty_r,
    dy_s,
    dy_r,
    sw_s,
    sw_r,
    e3_s,
    e3_r,
    e4_s,
    e4_r,
    e5_s,
    e5_r,
    cz_s,
    cz_r,
    cy_s,
    cy_r,
    cc_s,
    cc_r,
    gz_s,
    gz_r,
    gc_s,
    gc_r,
    op_s,
    op_r,
    nb_s,
    nb_r,
    z_s,
    z_r,
    across,
):
    p = lax.axis_index("pole")
    leaf = lax.axis_index("leaf")
    x = p // 4
    zh = p % 4
    y = leaf // 8
    e = leaf % 8
    zl = e // 2
    k = e % 2
    c = y // 2
    yp = y % 2
    y_mate = y + 1 - 2 * yp
    base = y * 8

    def copy(src, dst, ssem, rsem, pole_to, leaf_to):
        return pltpu.make_async_remote_copy(
            src_ref=src,
            dst_ref=dst,
            send_sem=ssem,
            recv_sem=rsem,
            device_id=(pole_to, leaf_to),
            device_id_type=MESH,
        )

    def arrived(dst, rsem):
        copy(dst, dst, rsem, rsem, p, leaf).wait_recv()

    def sent(src, ssem):
        copy(src, src, ssem, ssem, p, leaf).wait_send()

    barrier = pltpu.get_barrier_semaphore()

    def greet(pole_to, leaf_to):
        pl.semaphore_signal(barrier, inc=1, device_id=(pole_to, leaf_to), device_id_type=MESH)

    mate = base + e + 1 - 2 * k
    for t in (1, 3):
        greet(x * 4 + (zh + t) % 4, leaf)
    for t in (2, 1, 3):
        greet(p, (y + t) % 4 * 8 + e)
    for t in range(1, 4):
        greet(p, base + (e + 2 * t) % 8)
    greet((x + 1) % 4 * 4 + zh, leaf)
    greet((x + 3) % 4 * 4 + zh, leaf)
    greet(p, mate)

    loads = [
        pltpu.make_async_copy(root.at[0, 0], root_v.at[0:64], lsem.at[0]),
        pltpu.make_async_copy(root.at[0, 1], root_v.at[64:128], lsem.at[1]),
        pltpu.make_async_copy(fc.at[0], fc_v, lsem.at[2]),
        pltpu.make_async_copy(fg.at[0], fg_v, lsem.at[3]),
        pltpu.make_async_copy(dc.at[0, 0], diag_v.at[0, :, 0:128], lsem.at[4]),
        pltpu.make_async_copy(dc.at[0, 1], diag_v.at[0, :, 128:256], lsem.at[5]),
        pltpu.make_async_copy(dg.at[0, 0, :, 0:128], diag_v.at[1, :, 0:128], lsem.at[6]),
        pltpu.make_async_copy(dg.at[0, 1, :, 0:128], diag_v.at[1, :, 128:256], lsem.at[7]),
        pltpu.make_async_copy(sc_hbm, sc, lsem.at[8]),
        pltpu.make_async_copy(sg_hbm, sg, lsem.at[9]),
        pltpu.make_async_copy(pw_hbm, pw, lsem.at[10]),
        pltpu.make_async_copy(dg.at[0, 0, :, 128:256], diag_v.at[2, :, 0:128], lsem.at[11]),
        pltpu.make_async_copy(dg.at[0, 1, :, 128:256], diag_v.at[2, :, 128:256], lsem.at[12]),
    ]
    for i in (8, 9, 2, 3, 0, 1, 4, 5, 10, 6, 7, 11, 12):
        loads[i].start()

    own_c = pl.multiple_of((yp * 8 + e) * 128, 128)
    own_g = pl.multiple_of(e * 256, 256)
    loads[2].wait()
    ftc[pl.ds(own_c, 128), :] = transposed(fc_v, slice(0, 128))
    loads[3].wait()
    ftg[pl.ds(own_g, 128), :] = transposed(fg_v, slice(0, 128))
    ftg[pl.ds(pl.multiple_of(own_g + 128, 128), 128), :] = transposed(fg_v, slice(128, 256))

    loads[8].wait()
    loads[9].wait()
    loads[10].wait()
    child_rows = [sc[0:1, 0:128], twice(sc[0:1, 128:192]), sc[1:2, 0:128], twice(sc[1:2, 128:192])]
    hot_rows = jnp.concatenate(child_rows, axis=1).astype(F32)

    def build_hot(i, carry):
        at = pl.multiple_of(i * 128, 128)
        ids = iota((128, 512), 0) + (i * 128).astype(F32)
        oh[pl.ds(at, 128), :] = hot(ids == hot_rows)
        return carry

    lax.fori_loop(0, 16, build_hot, 0)
    loads[0].wait()
    loads[1].wait()
    taken = mm(root_v[...], oh[...])
    low_lanes = iota((64, 128), 1) < 64
    for ch in range(2):
        at = ch * 256
        t_send[ch, 0:64, :] = taken[0:64, at : at + 128].astype(BF)
        t_send[ch, 64:128, :] = taken[64:128, at : at + 128].astype(BF)
        t_send[ch, 128:192, :] = jnp.where(
            low_lanes, taken[0:64, at + 128 : at + 256], taken[64:128, at + 128 : at + 256]
        ).astype(BF)

    pl.semaphore_wait(barrier, 11)
    for t in (1, 3):
        pl.semaphore_signal(
            across, inc=1, device_id=(x * 4 + (zh + t) % 4, leaf), device_id_type=MESH
        )

    for t in range(1, 4):
        y_to = (y + t) % 4
        copy(t_send.at[y_to // 2], t_recv.at[y], ty_s.at[t - 1], ty_r.at[y], p, y_to * 8 + e).start()
    t_recv[pl.ds(y, 1)] = t_send[pl.ds(c, 1)]

    def c_block(yy, j, kk):
        return ftc.at[pl.ds(pl.multiple_of((yy * 8 + j * 2 + kk) * 128, 128), 128)]

    def g_block(j, kk, part_at):
        return ftg.at[pl.ds(pl.multiple_of((j * 2 + kk) * 256 + part_at * 128, 128), 128)]

    def c_up(j):
        return copy(c_block(yp, j, k), c_block(yp, j, k), cz_s.at[j], cz_r.at[j], p, base + e + 2)

    def c_down(j):
        return copy(c_block(yp, j, k), c_block(yp, j, k), cz_s.at[4 + j], cz_r.at[j], p, base + e - 2)

    def c_side(j):
        return copy(c_block(yp, j, k), c_block(yp, j, k), cy_s.at[j], cy_r.at[j], p, y_mate * 8 + e)

    def c_core(yy, j):
        i = yy * 4 + j
        return copy(c_block(yy, j, k), c_block(yy, j, k), cc_s.at[i], cc_r.at[i], p, base + e + 1 - 2 * k)

    def g_up(j, b):
        return copy(g_block(j, k, b), g_block(j, k, b), gz_s.at[0, b, j], gz_r.at[b, j], p, base + e + 2)

    def g_down(j, b):
        return copy(g_block(j, k, b), g_block(j, k, b), gz_s.at[1, b, j], gz_r.at[b, j], p, base + e - 2)

    def g_core(j, b):
        return copy(g_block(j, k, b), g_block(j, k, b), gc_s.at[b, j], gc_r.at[b, j], p, mate)

    def c_first():
        @pl.when(zl < 3)
        def _():
            c_up(zl).start()

        @pl.when(zl > 0)
        def _():
            c_down(zl).start()

        c_core(yp, zl).start()

    def g_first(b):
        @pl.when(zl < 3)
        def _():
            g_up(zl, b).start()

        @pl.when(zl > 0)
        def _():
            g_down(zl, b).start()

        g_core(zl, b).start()

    def c_relay(s):
        @pl.when(zl >= s)
        def _():
            j = zl - s
            arrived(c_block(yp, j, k), cz_r.at[j])

            @pl.when(zl < 3)
            def _():
                c_up(j).start()

            c_side(j).start()
            c_core(yp, j).start()

        @pl.when(zl + s <= 3)
        def _():
            j = zl + s
            arrived(c_block(yp, j, k), cz_r.at[j])

            @pl.when(zl > 0)
            def _():
                c_down(j).start()

            c_side(j).start()
            c_core(yp, j).start()

    def g_relay(s, b):
        @pl.when(zl >= s)
        def _():
            j = zl - s
            arrived(g_block(j, k, b), gz_r.at[b, j])

            @pl.when(zl < 3)
            def _():
                g_up(j, b).start()

            g_core(j, b).start()

        @pl.when(zl + s <= 3)
        def _():
            j = zl + s
            arrived(g_block(j, k, b), gz_r.at[b, j])

            @pl.when(zl > 0)
            def _():
                g_down(j, b).start()

            g_core(j, b).start()

    def c_finish():
        for i in range(4):
            arrived(c_block(1 - yp, i, k), cy_r.at[i])
            c_core(1 - yp, i).start()
        for i in range(8):
            arrived(c_block(i // 4, i % 4, 1 - k), cc_r.at[i])

    c_first()
    g_first(0)

    col0 = column(row_of(sg, y, slice(0, 128)))
    col1 = column(twice(row_of(sg, y, slice(128, 192))))
    col_mate = column(row_of(sg, y_mate, slice(0, 128)))
    lane = iota((128, 128), 1)

    def build_low(i, carry):
        at = pl.multiple_of(i * 128, 128)
        ids = lane + (i * 128).astype(F32)
        rl[0:128, pl.ds(at, 128)] = hot(col0 == ids)
        rl[128:256, pl.ds(at, 128)] = hot(col_mate == ids)
        return carry

    lax.fori_loop(0, 16, build_low, 0)
    loads[4].wait()
    loads[5].wait()
    picked = mm(rl[...], diag_v[0]).astype(BF)
    own_ids = iota((128, 128), 0) + own_c.astype(F32)
    pick_own = hot(own_ids == row_of(sg, y, slice(0, 128)).astype(F32))
    pick_mate = hot(own_ids == row_of(sg, y_mate, slice(0, 128)).astype(F32))
    d_send[0:96, :] = mm(picked[128:224, 0:128], pick_mate).astype(BF)
    d_send[96:192, :] = mm(picked[128:224, 128:256], pick_mate).astype(BF)
    copy(d_send, d_recv, dy_s.at[0], dy_r.at[0], p, y_mate * 8 + e).start()
    d_re = mm(picked[0:96, 0:128], pick_own)
    d_im = mm(picked[0:96, 128:256], pick_own)

    a_row0 = column(row_of(sc, c, slice(0, 128)))
    a_row1 = column(twice(row_of(sc, c, slice(128, 192))))
    lane_at = jnp.where(lane < 64, lane, lane + 448.0) + (e * 64).astype(F32)
    fold = jnp.concatenate(
        [
            jnp.concatenate([hot(a_row0 == lane_at), hot(a_row0 == lane_at + 1024.0)], axis=1),
            jnp.concatenate([hot(a_row1 == lane_at), hot(a_row1 == lane_at + 1024.0)], axis=1)[0:64],
        ],
        axis=0,
    )
    c_relay(1)
    for t in range(1, 4):
        y_from = (y + t) % 4
        arrived(t_recv.at[y_from], ty_r.at[y_from])
    for b in range(3):
        raw = jnp.concatenate([t_recv[i, b * 64 : b * 64 + 64, :] for i in range(4)], axis=0)
        part[b * 192 : b * 192 + 192, :] = mm(fold, raw).astype(BF)
    arrived(d_recv, dy_r.at[0])
    part[576:672, :] = (d_re + d_recv[0:96, :].astype(F32)).astype(BF)
    part[672:768, :] = (d_im + d_recv[96:192, :].astype(F32)).astype(BF)

    c_side(zl).start()

    def piece(ref, i):
        return ref.at[pl.ds(pl.multiple_of(i * 96, 96), 96)]

    def side_rows(kk):
        return pl.ds(pl.multiple_of(kk * 384, 128), 384)

    swap = copy(part.at[side_rows(1 - k)], sw_recv, sw_s.at[0], sw_r.at[0], p, mate)
    swap.start()
    arrived(sw_recv, sw_r.at[0])
    half[...] = (part[side_rows(k), :].astype(F32) + sw_recv[...].astype(F32)).astype(BF)

    for t in (2, 1, 3):
        to = (zl + t) % 4
        copy(piece(half, to), rs_recv.at[zl], e3_s.at[t - 1], e3_r.at[zl], p, base + to * 2 + k).start()
    c_relay(2)
    total = half[pl.ds(pl.multiple_of(zl * 96, 96), 96), :].astype(F32)
    for t in (1, 3, 2):
        at = (zl + t) % 4
        arrived(rs_recv.at[at], e3_r.at[at])
        total = total + rs_recv[at].astype(F32)
    mine = k * 4 + zl
    full[pl.ds(pl.multiple_of(mine * 96, 96), 96), :] = total.astype(BF)

    for t in (2, 1, 3):
        to = (zl + t) % 4
        copy(piece(full, mine), piece(full, mine), e4_s.at[t - 1], e4_r.at[zl], p, base + to * 2 + k).start()

    def to_mate(at):
        i = k * 4 + at
        copy(piece(full, i), piece(full, i), e5_s.at[at], e5_r.at[at], p, mate).start()

    to_mate(zl)
    g_first(1)
    c_relay(3)
    for t in (1, 3, 2):
        at = (zl + t) % 4
        arrived(piece(full, k * 4 + at), e4_r.at[at])
        to_mate(at)
    for at in range(4):
        arrived(piece(full, (1 - k) * 4 + at), e5_r.at[at])
    for b in range(3):
        acat[:, b * 128 : b * 128 + 128] = full[b * 192 : b * 192 + 192, :]

    g_relay(1, 0)
    g_relay(1, 1)
    g_re, g_im = right_side(fc_v[0], fc_v[1])
    a_now = acat[...]
    off_re = (-mm(a_now, g_re)).astype(BF)
    off_im = (-mm(a_now, g_im)).astype(BF)
    r_re, r_im = right_side(off_re, off_im)
    rhs[0, :, 0:128] = r_re
    rhs[0, :, 128:256] = r_im

    c_finish()

    w_im = pw[0, 0]
    w_re = pw[0, 1]
    x_next = (x + 1) % 4
    x_prev = (x + 3) % 4
    p_next = x_next * 4 + zh
    p_prev = x_prev * 4 + zh

    def process(i, quarter, role, b):
        at = b * 128
        ft_ref = ftc if i == 0 else ftg
        rows = [pl.ds(pl.multiple_of(quarter * 512 + h * 256 + at, 128), 128) for h in range(2)]
        ft = jnp.concatenate([ft_ref[r, :] for r in rows], axis=0)
        reduced = mm(ft, rhs[i])
        here = pl.ds(at, 128)
        for h in range(2):
            inverse = diag_v[i, rows[h], :].astype(F32) - reduced[h * 128 : h * 128 + 128]
            inverse = inverse.astype(BF).astype(F32)
            value = w_im * inverse[:, 128:256] + w_re * inverse[:, 0:128]
            dens[i, role, h, here] = value
            s_out[i, role, h, here] = value.astype(BF)

        @pl.when(role == 2)
        def _():
            opp_copy(i, 0, b, p_next).start()
            opp_copy(i, 1, b, p_prev).start()

        @pl.when(role == 1)
        def _():
            nb_copy(i, 0, 1, b).start()

        @pl.when(role == 3)
        def _():
            nb_copy(i, 1, 0, b).start()

    def opp_copy(i, h, b, to):
        here = pl.ds(b * 128, 128)
        return copy(s_out.at[i, 2, h, here], r_opp.at[i, h, here], op_s.at[i, h, b], op_r.at[i, h, b], to, leaf)

    def nb_copy(i, side, h, b):
        here = pl.ds(b * 128, 128)
        return copy(
            s_out.at[i, 1 + 2 * side, h, here],
            r_nb.at[i, side, h, here],
            nb_s.at[i, side, h, b],
            nb_r.at[i, side, h, b],
            p_prev if side else p_next,
            leaf,
        )

    def complete(i, b):
        here = pl.ds(b * 128, 128)
        for side in range(2):
            arrived(r_opp.at[i, side, here], op_r.at[i, side, b])
            s_out[i, 1 + 2 * side, side, here] = (
                dens[i, 1 + 2 * side, side, here] + r_opp[i, side, here].astype(F32)
            ).astype(BF)
            nb_copy(i, side, side, b).start()

    def z_copy(i, to):
        return copy(sz.at[i, to], rz.at[i, zh], z_s.at[i, to], z_r.at[i, zh], x * 4 + to, leaf)

    def along_z(i, b):
        here = pl.ds(b * 128, 128)
        for h in range(2):
            for side in range(2):
                arrived(r_nb.at[i, side, h, here], nb_r.at[i, side, h, b])
        for h in range(2):
            to = 2 * h + b
            total = dens[i, 0, h, here] + r_nb[i, 0, h, here].astype(F32) + r_nb[i, 1, h, here].astype(F32)

            @pl.when(zh != to)
            def _():
                sz[i, to] = total.astype(BF)
                z_copy(i, to).start()

            @pl.when(zh == to)
            def _():
                keep[i] = total

    def result(i):
        total = keep[i]
        for t in (1, 3, 2):
            z_from = (zh + t) % 4
            arrived(rz.at[i, z_from], z_r.at[i, z_from])
            total = total + rz[i, z_from].astype(F32)
        return total

    for b in range(2):
        for r in (2, 1, 3, 0):
            process(0, (x + r) % 4, r, b)

    ft_r = mm(rl[0:128, :], ftc[...])
    lane384 = lax.broadcasted_iota(jnp.int32, (128, 384), 1)
    is_im = ((lane384 >= 128) & (lane384 < 256)) | (lane384 >= 320)
    f_re = jnp.where(is_im, -ft_r, ft_r).astype(BF)
    f_im = jnp.concatenate(
        [ft_r[:, 128:256], ft_r[:, 0:128], pltpu.roll(ft_r[:, 256:384], 64, 1)], axis=1
    ).astype(BF)
    a_low = acat[0:128, :]
    a_high = jnp.concatenate([acat[128:192, :], acat[128:192, :]], axis=0)
    off_t = jnp.concatenate(
        [
            -mm_nt(f_re, a_low),
            -mm_nt(f_im, a_low),
            -jnp.where(lane < 64, mm_nt(f_re, a_high), mm_nt(f_im, a_high)),
        ],
        axis=1,
    ).astype(BF)
    none = jnp.zeros((128, 128), BF)
    up0 = col0 - 2048.0
    up1 = col1 - 2048.0
    lane_hi = jnp.where(lane < 64, lane, lane - 64.0) + 128.0
    near0 = hot(up0 == lane)
    near1 = hot(up1 == lane)
    far0 = up0 == lane_hi
    far1 = up1 == lane_hi
    sub = iota((128, 128), 0)
    q0 = jnp.concatenate([near0, none, hot(far0 & (lane < 64))], axis=1)
    q1 = jnp.concatenate([none, near0, hot(far0 & (lane >= 64))], axis=1)
    q2 = jnp.concatenate(
        [
            jnp.where(sub < 64, near1.astype(F32), 0.0).astype(BF),
            jnp.where(sub >= 64, near1.astype(F32), 0.0).astype(BF),
            hot(far1 & ((lane < 64) == (sub < 64))),
        ],
        axis=1,
    )
    up_near = jnp.concatenate([near0, near1[0:64]], axis=0)
    up_far = jnp.concatenate([hot(far0), hot(far1)[0:64]], axis=0)[:, 0:64]
    a_rows = mm(up_near, acat[0:128, :]) + mm(up_far, acat[128:192, :])
    rows_all = a_rows + jnp.concatenate([off_t.astype(F32), jnp.zeros((64, 384), F32)], axis=0)
    q_all = jnp.concatenate([q0, q1, q2], axis=0)
    ag = mm_nt(rows_all.astype(BF), q_all)
    up_re = jnp.concatenate([q0, q2[0:64]], axis=0)
    up_im = jnp.concatenate([q1, q2[64:128]], axis=0)
    rest = jnp.zeros((32, 128), F32)
    tail = jnp.zeros((64, 128), F32)
    in_re = jnp.concatenate([full[576:672, :].astype(F32), rest], axis=0) - mm_nt(f_re, off_t)
    in_im = jnp.concatenate([full[672:768, :].astype(F32), rest], axis=0) - mm_nt(f_im, off_t)
    agcat[:, 0:128] = (
        ag[:, 0:128] + mm_nt(up_re, off_t) + jnp.concatenate([in_re, tail], axis=0)
    ).astype(BF)
    agcat[:, 128:256] = (
        ag[:, 128:256] + mm_nt(up_im, off_t) + jnp.concatenate([in_im, tail], axis=0)
    ).astype(BF)
    agcat[:, 256:384] = ag[:, 256:384].astype(BF)


    g_relay(2, 0)
    g_relay(2, 1)
    gg_re, gg_im = right_side(fg_v[0], fg_v[1])
    ag_now = agcat[...]
    goff_re = (-mm(ag_now, gg_re)).astype(BF)
    goff_im = (-mm(ag_now, gg_im)).astype(BF)
    r_re, r_im = right_side(goff_re, goff_im)
    for h in range(2):
        rhs[1 + h, :, 0:128] = r_re[:, h * 128 : h * 128 + 128]
        rhs[1 + h, :, 128:256] = r_im[:, h * 128 : h * 128 + 128]

    def g_quarter(q, b):
        arrived(g_block(q, 1 - k, b), gc_r.at[b, q])
        role = (q - x + 4) % 4
        process(1, q, role, b)
        process(2, q, role, b)

    for i in (6, 7, 11, 12):
        loads[i].wait()
    pl.semaphore_wait(across, 2)
    far = 3 * (1 - zl // 2)
    for b in range(2):
        g_quarter(zl, b)
    for b in range(2):
        complete(0, b)
    for b in range(2):
        g_quarter(zl + 1 - 2 * (zl // 2), b)
    for b in range(2):
        g_quarter((3 * zl + 2) % 5, b)
    for b in range(2):
        along_z(0, b)
    for b in range(2):
        g_relay(3, b)
        g_quarter(far, b)
    for b in range(2):
        for i in (1, 2):
            complete(i, b)
    for b in range(2):
        for i in (1, 2):
            along_z(i, b)
    out_c[...] = result(0)
    out_g[:, 0:128] = result(1)
    out_g[:, 128:256] = result(2)

    for t in range(3):
        sent(t_send.at[0], ty_s.at[t])
    for i in range(3):
        for to in range(4):

            @pl.when(zh != to)
            def _(i=i, to=to):
                sent(sz.at[0, 0], z_s.at[i, to])

        for b in range(2):
            for h in range(2):
                sent(sz.at[0, 0], op_s.at[i, h, b])
                for side in range(2):
                    sent(sz.at[0, 0], nb_s.at[i, side, h, b])
    sent(d_send, dy_s.at[0])
    sent(sw_recv, sw_s.at[0])
    for t in range(3):
        sent(piece(half, 0), e3_s.at[t])
        sent(piece(full, 0), e4_s.at[t])
    for t in range(4):
        sent(piece(full, 0), e5_s.at[t])
    for j in range(4):

        @pl.when((zl < 3) & (j <= zl))
        def _(j=j):
            sent(c_block(0, 0, 0), cz_s.at[j])
            for b in range(2):
                sent(g_block(0, 0, 0), gz_s.at[0, b, j])

        @pl.when((zl > 0) & (j >= zl))
        def _(j=j):
            sent(c_block(0, 0, 0), cz_s.at[4 + j])
            for b in range(2):
                sent(g_block(0, 0, 0), gz_s.at[1, b, j])

        sent(c_block(0, 0, 0), cy_s.at[j])
        sent(c_block(0, 0, 0), cc_s.at[j])
        sent(c_block(0, 0, 0), cc_s.at[4 + j])
        for b in range(2):
            sent(g_block(0, 0, 0), gc_s.at[b, j])


def local(*args):
    vm = pltpu.VMEM
    dma = pltpu.SemaphoreType.DMA
    scratch = [
        vm((2, 192), jnp.int32),
        vm((4, 192), jnp.int32),
        pltpu.SMEM((1, 2), F32),
        vm((128, 2048), BF),
        vm((2, 192, 128), BF),
        vm((2, 192, 256), BF),
        vm((3, 2048, 256), BF),
        vm((2048, 384), BF),
        vm((2048, 384), BF),
        vm((2048, 512), BF),
        vm((256, 2048), BF),
        vm((2, 192, 128), BF),
        vm((4, 192, 128), BF),
        vm((192, 128), BF),
        vm((192, 128), BF),
        vm((768, 128), BF),
        vm((384, 128), BF),
        vm((384, 128), BF),
        vm((4, 96, 128), BF),
        vm((768, 128), BF),
        vm((192, 384), BF),
        vm((192, 384), BF),
        vm((3, 384, 256), BF),
        vm((3, 4, 2, 256, 128), BF),
        vm((3, 2, 256, 128), BF),
        vm((3, 2, 2, 256, 128), BF),
        vm((3, 4, 2, 256, 128), F32),
        vm((3, 4, 128, 128), BF),
        vm((3, 4, 128, 128), BF),
        vm((3, 128, 128), F32),
        dma((13,)),
        dma((3,)),
        dma((4,)),
        dma((1,)),
        dma((1,)),
        dma((1,)),
        dma((1,)),
        dma((3,)),
        dma((4,)),
        dma((3,)),
        dma((4,)),
        dma((4,)),
        dma((4,)),
        dma((8,)),
        dma((4,)),
        dma((4,)),
        dma((4,)),
        dma((8,)),
        dma((8,)),
        dma((2, 2, 4)),
        dma((2, 4)),
        dma((2, 4)),
        dma((2, 4)),
        dma((3, 2, 2)),
        dma((3, 2, 2)),
        dma((3, 2, 2, 2)),
        dma((3, 2, 2, 2)),
        dma((3, 4)),
        dma((3, 4)),
        pltpu.SemaphoreType.REGULAR,
    ]
    hbm = pl.BlockSpec(memory_space=pltpu.HBM)
    vm_spec = pl.BlockSpec(memory_space=pltpu.VMEM)
    return pl.pallas_call(
        kernel,
        out_shape=[
            pltpu.VMEM((128, 128), F32),
            pltpu.VMEM((128, 256), F32),
        ],
        in_specs=[hbm] * 8,
        out_specs=[vm_spec, vm_spec],
        scratch_shapes=scratch,
        compiler_params=pltpu.CompilerParams(
            collective_id=0, has_side_effects=True, vmem_limit_bytes=60 * 1024 * 1024
        ),
        cost_estimate=pl.CostEstimate(flops=3_000_000_000, bytes_accessed=5_000_000, transcendentals=0),
    )(*args)


def solution(mesh):
    placed = (
        P("pole", None, "leaf", None),
        P("pole", None, None, "leaf"),
        P("pole", None, None, "leaf"),
        P("pole", None, None, "leaf"),
        P("pole", None, None, "leaf"),
        P(),
        P(),
        P("pole", None),
    )
    return jax.shard_map(
        local,
        mesh=mesh,
        in_specs=placed,
        out_specs=(P("pole", "leaf"), P("pole", "leaf")),
        check_vma=False,
    )
```

```python
import jax
import jax.numpy as jnp
from jax import lax
from jax.experimental import pallas as pl
from jax.experimental.pallas import tpu as pltpu
from jax.sharding import PartitionSpec as P

MESH = pl.DeviceIdType.MESH
BF = jnp.bfloat16
F32 = jnp.float32


def mm(a, b):
    return jnp.dot(a, b, preferred_element_type=F32)


def mm_nt(a, b):
    return lax.dot_general(a, b, (((1,), (1,)), ((), ())), preferred_element_type=F32)


def hot(cond):
    return jnp.where(cond, 1.0, 0.0).astype(BF)


def column(row):
    return jnp.transpose(jnp.broadcast_to(row.astype(F32), (128, 128)))


def iota(shape, dim):
    return lax.broadcasted_iota(jnp.int32, shape, dim).astype(F32)


def twice(row):
    return jnp.concatenate([row, row], axis=1)


def row_of(ref, index, lanes):
    row = ref[0:1, lanes]
    for i in range(1, ref.shape[0]):
        row = jnp.where(index == i, ref[i : i + 1, lanes], row)
    return row


def right_side(off_re, off_im):
    re_col = jnp.concatenate([off_re[:128], -off_im[:128], off_re[128:], -off_im[128:]], axis=0)
    im_col = jnp.concatenate([off_im[:128], off_re[:128], off_im[128:], off_re[128:]], axis=0)
    return re_col, im_col


def transposed(ref, cols):
    parts = [
        ref[0, 0:128, cols],
        ref[1, 0:128, cols],
        jnp.concatenate([ref[0, 128:192, cols], ref[1, 128:192, cols]], axis=0),
    ]
    return jnp.concatenate([jnp.transpose(p.astype(F32)) for p in parts], axis=1).astype(BF)


def kernel(
    root,
    fc,
    fg,
    dc,
    dg,
    sc_hbm,
    sg_hbm,
    pw_hbm,
    out_c,
    out_g,
    sc,
    sg,
    pw,
    root_v,
    fc_v,
    fg_v,
    diag_v,
    ftc,
    ftg,
    oh,
    rl,
    t_send,
    t_recv,
    d_send,
    d_recv,
    part,
    sw_recv,
    half,
    rs_recv,
    full,
    acat,
    agcat,
    rhs,
    s_out,
    r_opp,
    r_nb,
    dens,
    sz,
    rz,
    keep,
    lsem,
    ty_s,
    ty_r,
    dy_s,
    dy_r,
    sw_s,
    sw_r,
    e3_s,
    e3_r,
    e4_s,
    e4_r,
    e5_s,
    e5_r,
    cz_s,
    cz_r,
    cy_s,
    cy_r,
    cc_s,
    cc_r,
    gz_s,
    gz_r,
    gc_s,
    gc_r,
    op_s,
    op_r,
    nb_s,
    nb_r,
    z_s,
    z_r,
    across,
):
    p = lax.axis_index("pole")
    leaf = lax.axis_index("leaf")
    x = p // 4
    zh = p % 4
    y = leaf // 8
    e = leaf % 8
    zl = e // 2
    k = e % 2
    c = y // 2
    yp = y % 2
    y_mate = y + 1 - 2 * yp
    base = y * 8

    def copy(src, dst, ssem, rsem, pole_to, leaf_to):
        return pltpu.make_async_remote_copy(
            src_ref=src,
            dst_ref=dst,
            send_sem=ssem,
            recv_sem=rsem,
            device_id=(pole_to, leaf_to),
            device_id_type=MESH,
        )

    def arrived(dst, rsem):
        copy(dst, dst, rsem, rsem, p, leaf).wait_recv()

    def sent(src, ssem):
        copy(src, src, ssem, ssem, p, leaf).wait_send()

    barrier = pltpu.get_barrier_semaphore()

    def greet(pole_to, leaf_to):
        pl.semaphore_signal(barrier, inc=1, device_id=(pole_to, leaf_to), device_id_type=MESH)

    mate = base + e + 1 - 2 * k
    for t in (1, 3):
        greet(x * 4 + (zh + t) % 4, leaf)
    for t in (2, 1, 3):
        greet(p, (y + t) % 4 * 8 + e)
    for t in range(1, 4):
        greet(p, base + (e + 2 * t) % 8)
    greet((x + 1) % 4 * 4 + zh, leaf)
    greet((x + 3) % 4 * 4 + zh, leaf)
    greet(p, mate)

    loads = [
        pltpu.make_async_copy(root.at[0, 0], root_v.at[0:64], lsem.at[0]),
        pltpu.make_async_copy(root.at[0, 1], root_v.at[64:128], lsem.at[1]),
        pltpu.make_async_copy(fc.at[0], fc_v, lsem.at[2]),
        pltpu.make_async_copy(fg.at[0], fg_v, lsem.at[3]),
        pltpu.make_async_copy(dc.at[0, 0], diag_v.at[0, :, 0:128], lsem.at[4]),
        pltpu.make_async_copy(dc.at[0, 1], diag_v.at[0, :, 128:256], lsem.at[5]),
        pltpu.make_async_copy(dg.at[0, 0, :, 0:128], diag_v.at[1, :, 0:128], lsem.at[6]),
        pltpu.make_async_copy(dg.at[0, 1, :, 0:128], diag_v.at[1, :, 128:256], lsem.at[7]),
        pltpu.make_async_copy(sc_hbm, sc, lsem.at[8]),
        pltpu.make_async_copy(sg_hbm, sg, lsem.at[9]),
        pltpu.make_async_copy(pw_hbm, pw, lsem.at[10]),
        pltpu.make_async_copy(dg.at[0, 0, :, 128:256], diag_v.at[2, :, 0:128], lsem.at[11]),
        pltpu.make_async_copy(dg.at[0, 1, :, 128:256], diag_v.at[2, :, 128:256], lsem.at[12]),
    ]
    for i in (8, 9, 2, 3, 0, 1, 4, 5, 10, 6, 7, 11, 12):
        loads[i].start()

    own_c = pl.multiple_of((yp * 8 + e) * 128, 128)
    own_g = pl.multiple_of(e * 256, 256)
    loads[2].wait()
    ftc[pl.ds(own_c, 128), :] = transposed(fc_v, slice(0, 128))
    loads[3].wait()
    ftg[pl.ds(own_g, 128), :] = transposed(fg_v, slice(0, 128))

    loads[8].wait()
    loads[9].wait()
    loads[10].wait()
    high = jnp.concatenate([sc[0:1, 128:192], sc[1:2, 128:192]], axis=1)
    child_rows = [sc[0:1, 0:128], sc[1:2, 0:128], high]
    hot_rows = jnp.concatenate(child_rows, axis=1).astype(F32)

    def build_hot(i, carry):
        at = pl.multiple_of(i * 128, 128)
        ids = iota((128, 384), 0) + (i * 128).astype(F32)
        oh[pl.ds(at, 128), :] = hot(ids == hot_rows)
        return carry

    lax.fori_loop(0, 16, build_hot, 0)
    loads[0].wait()
    loads[1].wait()
    taken = mm(root_v[...], oh[...])
    low_lanes = iota((64, 128), 1) < 64
    high_re = taken[0:64, 256:384]
    high_im = taken[64:128, 256:384]
    for ch in range(2):
        at = ch * 128
        t_send[ch, 0:64, :] = taken[0:64, at : at + 128].astype(BF)
        t_send[ch, 64:128, :] = taken[64:128, at : at + 128].astype(BF)
    t_send[0, 128:192, :] = jnp.where(low_lanes, high_re, pltpu.roll(high_im, 64, 1)).astype(BF)
    t_send[1, 128:192, :] = jnp.where(low_lanes, pltpu.roll(high_re, 64, 1), high_im).astype(BF)

    pl.semaphore_wait(barrier, 11)
    for t in (1, 3):
        pl.semaphore_signal(
            across, inc=1, device_id=(x * 4 + (zh + t) % 4, leaf), device_id_type=MESH
        )

    for t in range(1, 4):
        y_to = (y + t) % 4
        copy(t_send.at[y_to // 2], t_recv.at[y], ty_s.at[t - 1], ty_r.at[y], p, y_to * 8 + e).start()
    t_recv[pl.ds(y, 1)] = t_send[pl.ds(c, 1)]

    def c_block(yy, j, kk):
        return ftc.at[pl.ds(pl.multiple_of((yy * 8 + j * 2 + kk) * 128, 128), 128)]

    def g_block(j, kk, part_at):
        return ftg.at[pl.ds(pl.multiple_of((j * 2 + kk) * 256 + part_at * 128, 128), 128)]

    def c_up(j):
        return copy(c_block(yp, j, k), c_block(yp, j, k), cz_s.at[j], cz_r.at[j], p, base + e + 2)

    def c_down(j):
        return copy(c_block(yp, j, k), c_block(yp, j, k), cz_s.at[4 + j], cz_r.at[j], p, base + e - 2)

    def c_side(j):
        return copy(c_block(yp, j, k), c_block(yp, j, k), cy_s.at[j], cy_r.at[j], p, y_mate * 8 + e)

    def c_core(yy, j):
        i = yy * 4 + j
        return copy(c_block(yy, j, k), c_block(yy, j, k), cc_s.at[i], cc_r.at[i], p, base + e + 1 - 2 * k)

    def g_up(j, b):
        return copy(g_block(j, k, b), g_block(j, k, b), gz_s.at[0, b, j], gz_r.at[b, j], p, base + e + 2)

    def g_down(j, b):
        return copy(g_block(j, k, b), g_block(j, k, b), gz_s.at[1, b, j], gz_r.at[b, j], p, base + e - 2)

    def g_core(j, b):
        return copy(g_block(j, k, b), g_block(j, k, b), gc_s.at[b, j], gc_r.at[b, j], p, mate)

    def c_first():
        @pl.when(zl < 3)
        def _():
            c_up(zl).start()

        @pl.when(zl > 0)
        def _():
            c_down(zl).start()

        c_core(yp, zl).start()

    def g_first(b):
        @pl.when(zl < 3)
        def _():
            g_up(zl, b).start()

        @pl.when(zl > 0)
        def _():
            g_down(zl, b).start()

        g_core(zl, b).start()

    def c_relay(s):
        @pl.when(zl >= s)
        def _():
            j = zl - s
            arrived(c_block(yp, j, k), cz_r.at[j])

            @pl.when(zl < 3)
            def _():
                c_up(j).start()

            c_side(j).start()
            c_core(yp, j).start()

        @pl.when(zl + s <= 3)
        def _():
            j = zl + s
            arrived(c_block(yp, j, k), cz_r.at[j])

            @pl.when(zl > 0)
            def _():
                c_down(j).start()

            c_side(j).start()
            c_core(yp, j).start()

    def g_relay(s, b):
        @pl.when(zl >= s)
        def _():
            j = zl - s
            arrived(g_block(j, k, b), gz_r.at[b, j])

            @pl.when(zl < 3)
            def _():
                g_up(j, b).start()

            g_core(j, b).start()

        @pl.when(zl + s <= 3)
        def _():
            j = zl + s
            arrived(g_block(j, k, b), gz_r.at[b, j])

            @pl.when(zl > 0)
            def _():
                g_down(j, b).start()

            g_core(j, b).start()

    def c_finish():
        for i in range(4):
            arrived(c_block(1 - yp, i, k), cy_r.at[i])
            c_core(1 - yp, i).start()
        for i in range(8):
            arrived(c_block(i // 4, i % 4, 1 - k), cc_r.at[i])

    c_first()
    g_first(0)
    ftg[pl.ds(pl.multiple_of(own_g + 128, 128), 128), :] = transposed(fg_v, slice(128, 256))

    col0 = column(row_of(sg, y, slice(0, 128)))
    col1 = column(twice(row_of(sg, y, slice(128, 192))))
    col_mate = column(row_of(sg, y_mate, slice(0, 128)))
    lane = iota((128, 128), 1)

    def build_low(i, carry):
        at = pl.multiple_of(i * 128, 128)
        ids = lane + (i * 128).astype(F32)
        rl[0:128, pl.ds(at, 128)] = hot(col0 == ids)
        rl[128:256, pl.ds(at, 128)] = hot(col_mate == ids)
        return carry

    lax.fori_loop(0, 16, build_low, 0)
    loads[4].wait()
    loads[5].wait()
    picked = mm(rl[...], diag_v[0]).astype(BF)
    own_ids = iota((128, 128), 0) + own_c.astype(F32)
    pick_own = hot(own_ids == row_of(sg, y, slice(0, 128)).astype(F32))
    pick_mate = hot(own_ids == row_of(sg, y_mate, slice(0, 128)).astype(F32))
    d_send[0:96, :] = mm(picked[128:224, 0:128], pick_mate).astype(BF)
    d_send[96:192, :] = mm(picked[128:224, 128:256], pick_mate).astype(BF)
    copy(d_send, d_recv, dy_s.at[0], dy_r.at[0], p, y_mate * 8 + e).start()
    d_re = mm(picked[0:96, 0:128], pick_own)
    d_im = mm(picked[0:96, 128:256], pick_own)

    a_row0 = column(row_of(sc, c, slice(0, 128)))
    a_row1 = column(twice(row_of(sc, c, slice(128, 192))))
    lane_at = jnp.where(lane < 64, lane, lane + 448.0) + (e * 64).astype(F32)
    fold = jnp.concatenate(
        [
            jnp.concatenate([hot(a_row0 == lane_at), hot(a_row0 == lane_at + 1024.0)], axis=1),
            jnp.concatenate([hot(a_row1 == lane_at), hot(a_row1 == lane_at + 1024.0)], axis=1)[0:64],
        ],
        axis=0,
    )
    c_relay(1)
    for t in range(1, 4):
        y_from = (y + t) % 4
        arrived(t_recv.at[y_from], ty_r.at[y_from])
    for b in range(3):
        raw = jnp.concatenate([t_recv[i, b * 64 : b * 64 + 64, :] for i in range(4)], axis=0)
        part[b * 192 : b * 192 + 192, :] = mm(fold, raw).astype(BF)
    arrived(d_recv, dy_r.at[0])
    part[576:672, :] = (d_re + d_recv[0:96, :].astype(F32)).astype(BF)
    part[672:768, :] = (d_im + d_recv[96:192, :].astype(F32)).astype(BF)

    c_side(zl).start()

    def piece(ref, i):
        return ref.at[pl.ds(pl.multiple_of(i * 96, 96), 96)]

    def side_rows(kk):
        return pl.ds(pl.multiple_of(kk * 384, 128), 384)

    swap = copy(part.at[side_rows(1 - k)], sw_recv, sw_s.at[0], sw_r.at[0], p, mate)
    swap.start()
    arrived(sw_recv, sw_r.at[0])
    half[...] = (part[side_rows(k), :].astype(F32) + sw_recv[...].astype(F32)).astype(BF)

    for t in (2, 1, 3):
        to = (zl + t) % 4
        copy(piece(half, to), rs_recv.at[zl], e3_s.at[t - 1], e3_r.at[zl], p, base + to * 2 + k).start()
    c_relay(2)
    total = half[pl.ds(pl.multiple_of(zl * 96, 96), 96), :].astype(F32)
    for t in (1, 3, 2):
        at = (zl + t) % 4
        arrived(rs_recv.at[at], e3_r.at[at])
        total = total + rs_recv[at].astype(F32)
    mine = k * 4 + zl
    full[pl.ds(pl.multiple_of(mine * 96, 96), 96), :] = total.astype(BF)

    for t in (2, 1, 3):
        to = (zl + t) % 4
        copy(piece(full, mine), piece(full, mine), e4_s.at[t - 1], e4_r.at[zl], p, base + to * 2 + k).start()

    def to_mate(at):
        i = k * 4 + at
        copy(piece(full, i), piece(full, i), e5_s.at[at], e5_r.at[at], p, mate).start()

    to_mate(zl)
    g_first(1)
    c_relay(3)
    for t in (1, 3, 2):
        at = (zl + t) % 4
        arrived(piece(full, k * 4 + at), e4_r.at[at])
        to_mate(at)
    for at in range(4):
        arrived(piece(full, (1 - k) * 4 + at), e5_r.at[at])
    for b in range(3):
        acat[:, b * 128 : b * 128 + 128] = full[b * 192 : b * 192 + 192, :]

    g_relay(1, 0)
    g_relay(1, 1)
    g_re, g_im = right_side(fc_v[0], fc_v[1])
    a_now = acat[...]
    off_re = (-mm(a_now, g_re)).astype(BF)
    off_im = (-mm(a_now, g_im)).astype(BF)
    r_re, r_im = right_side(off_re, off_im)
    rhs[0, :, 0:128] = r_re
    rhs[0, :, 128:256] = r_im

    c_finish()

    w_im = pw[0, 0]
    w_re = pw[0, 1]
    x_next = (x + 1) % 4
    x_prev = (x + 3) % 4
    p_next = x_next * 4 + zh
    p_prev = x_prev * 4 + zh

    def process(i, quarter, role, b):
        at = b * 128
        ft_ref = ftc if i == 0 else ftg
        rows = [pl.ds(pl.multiple_of(quarter * 512 + h * 256 + at, 128), 128) for h in range(2)]
        ft = jnp.concatenate([ft_ref[r, :] for r in rows], axis=0)
        reduced = mm(ft, rhs[i])
        here = pl.ds(at, 128)
        for h in range(2):
            inverse = diag_v[i, rows[h], :].astype(F32) - reduced[h * 128 : h * 128 + 128]
            inverse = inverse.astype(BF).astype(F32)
            value = w_im * inverse[:, 128:256] + w_re * inverse[:, 0:128]
            dens[i, role, h, here] = value
            s_out[i, role, h, here] = value.astype(BF)

        @pl.when(role == 2)
        def _():
            opp_copy(i, 0, b, p_next).start()
            opp_copy(i, 1, b, p_prev).start()

        @pl.when(role == 1)
        def _():
            nb_copy(i, 0, 1, b).start()

        @pl.when(role == 3)
        def _():
            nb_copy(i, 1, 0, b).start()

    def opp_copy(i, h, b, to):
        here = pl.ds(b * 128, 128)
        return copy(s_out.at[i, 2, h, here], r_opp.at[i, h, here], op_s.at[i, h, b], op_r.at[i, h, b], to, leaf)

    def nb_copy(i, side, h, b):
        here = pl.ds(b * 128, 128)
        return copy(
            s_out.at[i, 1 + 2 * side, h, here],
            r_nb.at[i, side, h, here],
            nb_s.at[i, side, h, b],
            nb_r.at[i, side, h, b],
            p_prev if side else p_next,
            leaf,
        )

    def complete(i, b):
        here = pl.ds(b * 128, 128)
        for side in range(2):
            arrived(r_opp.at[i, side, here], op_r.at[i, side, b])
            s_out[i, 1 + 2 * side, side, here] = (
                dens[i, 1 + 2 * side, side, here] + r_opp[i, side, here].astype(F32)
            ).astype(BF)
            nb_copy(i, side, side, b).start()

    def z_copy(i, to):
        return copy(sz.at[i, to], rz.at[i, zh], z_s.at[i, to], z_r.at[i, zh], x * 4 + to, leaf)

    def along_z(i, b):
        here = pl.ds(b * 128, 128)
        for h in range(2):
            for side in range(2):
                arrived(r_nb.at[i, side, h, here], nb_r.at[i, side, h, b])
        for h in range(2):
            to = 2 * h + b
            total = dens[i, 0, h, here] + r_nb[i, 0, h, here].astype(F32) + r_nb[i, 1, h, here].astype(F32)

            @pl.when(zh != to)
            def _():
                sz[i, to] = total.astype(BF)
                z_copy(i, to).start()

            @pl.when(zh == to)
            def _():
                keep[i] = total

    def result(i):
        total = keep[i]
        for t in (1, 3, 2):
            z_from = (zh + t) % 4
            arrived(rz.at[i, z_from], z_r.at[i, z_from])
            total = total + rz[i, z_from].astype(F32)
        return total

    for b in range(2):
        for r in (2, 1, 3, 0):
            process(0, (x + r) % 4, r, b)

    ft_r = mm(rl[0:128, :], ftc[...])
    lane384 = lax.broadcasted_iota(jnp.int32, (128, 384), 1)
    is_im = ((lane384 >= 128) & (lane384 < 256)) | (lane384 >= 320)
    f_re = jnp.where(is_im, -ft_r, ft_r).astype(BF)
    f_im = jnp.concatenate(
        [ft_r[:, 128:256], ft_r[:, 0:128], pltpu.roll(ft_r[:, 256:384], 64, 1)], axis=1
    ).astype(BF)
    a_low = acat[0:128, :]
    a_high = jnp.concatenate([acat[128:192, :], acat[128:192, :]], axis=0)
    off_t = jnp.concatenate(
        [
            -mm_nt(f_re, a_low),
            -mm_nt(f_im, a_low),
            -jnp.where(lane < 64, mm_nt(f_re, a_high), mm_nt(f_im, a_high)),
        ],
        axis=1,
    ).astype(BF)
    none = jnp.zeros((128, 128), BF)
    up0 = col0 - 2048.0
    up1 = col1 - 2048.0
    lane_hi = jnp.where(lane < 64, lane, lane - 64.0) + 128.0
    near0 = hot(up0 == lane)
    near1 = hot(up1 == lane)
    far0 = up0 == lane_hi
    far1 = up1 == lane_hi
    sub = iota((128, 128), 0)
    q0 = jnp.concatenate([near0, none, hot(far0 & (lane < 64))], axis=1)
    q1 = jnp.concatenate([none, near0, hot(far0 & (lane >= 64))], axis=1)
    q2 = jnp.concatenate(
        [
            jnp.where(sub < 64, near1.astype(F32), 0.0).astype(BF),
            jnp.where(sub >= 64, near1.astype(F32), 0.0).astype(BF),
            hot(far1 & ((lane < 64) == (sub < 64))),
        ],
        axis=1,
    )
    up_near = jnp.concatenate([near0, near1[0:64]], axis=0)
    up_far = jnp.concatenate([hot(far0), hot(far1)[0:64]], axis=0)[:, 0:64]
    a_rows = mm(up_near, acat[0:128, :]) + mm(up_far, acat[128:192, :])
    rows_all = a_rows + jnp.concatenate([off_t.astype(F32), jnp.zeros((64, 384), F32)], axis=0)
    q_all = jnp.concatenate([q0, q1, q2], axis=0)
    ag = mm_nt(rows_all.astype(BF), q_all)
    up_re = jnp.concatenate([q0, q2[0:64]], axis=0)
    up_im = jnp.concatenate([q1, q2[64:128]], axis=0)
    rest = jnp.zeros((32, 128), F32)
    tail = jnp.zeros((64, 128), F32)
    in_re = jnp.concatenate([full[576:672, :].astype(F32), rest], axis=0) - mm_nt(f_re, off_t)
    in_im = jnp.concatenate([full[672:768, :].astype(F32), rest], axis=0) - mm_nt(f_im, off_t)
    agcat[:, 0:128] = (
        ag[:, 0:128] + mm_nt(up_re, off_t) + jnp.concatenate([in_re, tail], axis=0)
    ).astype(BF)
    agcat[:, 128:256] = (
        ag[:, 128:256] + mm_nt(up_im, off_t) + jnp.concatenate([in_im, tail], axis=0)
    ).astype(BF)
    agcat[:, 256:384] = ag[:, 256:384].astype(BF)


    g_relay(2, 0)
    g_relay(2, 1)
    gg_re, gg_im = right_side(fg_v[0], fg_v[1])
    ag_now = agcat[...]
    goff_re = (-mm(ag_now, gg_re)).astype(BF)
    goff_im = (-mm(ag_now, gg_im)).astype(BF)
    r_re, r_im = right_side(goff_re, goff_im)
    for h in range(2):
        rhs[1 + h, :, 0:128] = r_re[:, h * 128 : h * 128 + 128]
        rhs[1 + h, :, 128:256] = r_im[:, h * 128 : h * 128 + 128]

    def g_quarter(q, b):
        arrived(g_block(q, 1 - k, b), gc_r.at[b, q])
        role = (q - x + 4) % 4
        process(1, q, role, b)
        process(2, q, role, b)

    for i in (6, 7, 11, 12):
        loads[i].wait()
    pl.semaphore_wait(across, 2)
    far = 3 * (1 - zl // 2)
    for b in range(2):
        g_quarter(zl, b)
    for b in range(2):
        complete(0, b)
    for b in range(2):
        g_quarter(zl + 1 - 2 * (zl // 2), b)
    for b in range(2):
        g_quarter((3 * zl + 2) % 5, b)
    for b in range(2):
        along_z(0, b)
    for b in range(2):
        g_relay(3, b)
        g_quarter(far, b)
    for b in range(2):
        for i in (1, 2):
            complete(i, b)
    for b in range(2):
        for i in (1, 2):
            along_z(i, b)
    for t in range(3):
        sent(t_send.at[0], ty_s.at[t])
    for i in range(3):
        for b in range(2):
            for h in range(2):
                sent(sz.at[0, 0], op_s.at[i, h, b])
                for side in range(2):
                    sent(sz.at[0, 0], nb_s.at[i, side, h, b])
    sent(d_send, dy_s.at[0])
    sent(sw_recv, sw_s.at[0])
    for t in range(3):
        sent(piece(half, 0), e3_s.at[t])
        sent(piece(full, 0), e4_s.at[t])
    for t in range(4):
        sent(piece(full, 0), e5_s.at[t])
    for j in range(4):

        @pl.when((zl < 3) & (j <= zl))
        def _(j=j):
            sent(c_block(0, 0, 0), cz_s.at[j])
            for b in range(2):
                sent(g_block(0, 0, 0), gz_s.at[0, b, j])

        @pl.when((zl > 0) & (j >= zl))
        def _(j=j):
            sent(c_block(0, 0, 0), cz_s.at[4 + j])
            for b in range(2):
                sent(g_block(0, 0, 0), gz_s.at[1, b, j])

        sent(c_block(0, 0, 0), cy_s.at[j])
        sent(c_block(0, 0, 0), cc_s.at[j])
        sent(c_block(0, 0, 0), cc_s.at[4 + j])
        for b in range(2):
            sent(g_block(0, 0, 0), gc_s.at[b, j])

    out_c[...] = result(0)
    out_g[:, 0:128] = result(1)
    out_g[:, 128:256] = result(2)
    for i in range(3):
        for to in range(4):

            @pl.when(zh != to)
            def _(i=i, to=to):
                sent(sz.at[0, 0], z_s.at[i, to])


def local(*args):
    vm = pltpu.VMEM
    dma = pltpu.SemaphoreType.DMA
    scratch = [
        vm((2, 192), jnp.int32),
        vm((4, 192), jnp.int32),
        pltpu.SMEM((1, 2), F32),
        vm((128, 2048), BF),
        vm((2, 192, 128), BF),
        vm((2, 192, 256), BF),
        vm((3, 2048, 256), BF),
        vm((2048, 384), BF),
        vm((2048, 384), BF),
        vm((2048, 384), BF),
        vm((256, 2048), BF),
        vm((2, 192, 128), BF),
        vm((4, 192, 128), BF),
        vm((192, 128), BF),
        vm((192, 128), BF),
        vm((768, 128), BF),
        vm((384, 128), BF),
        vm((384, 128), BF),
        vm((4, 96, 128), BF),
        vm((768, 128), BF),
        vm((192, 384), BF),
        vm((192, 384), BF),
        vm((3, 384, 256), BF),
        vm((3, 4, 2, 256, 128), BF),
        vm((3, 2, 256, 128), BF),
        vm((3, 2, 2, 256, 128), BF),
        vm((3, 4, 2, 256, 128), F32),
        vm((3, 4, 128, 128), BF),
        vm((3, 4, 128, 128), BF),
        vm((3, 128, 128), F32),
        dma((13,)),
        dma((3,)),
        dma((4,)),
        dma((1,)),
        dma((1,)),
        dma((1,)),
        dma((1,)),
        dma((3,)),
        dma((4,)),
        dma((3,)),
        dma((4,)),
        dma((4,)),
        dma((4,)),
        dma((8,)),
        dma((4,)),
        dma((4,)),
        dma((4,)),
        dma((8,)),
        dma((8,)),
        dma((2, 2, 4)),
        dma((2, 4)),
        dma((2, 4)),
        dma((2, 4)),
        dma((3, 2, 2)),
        dma((3, 2, 2)),
        dma((3, 2, 2, 2)),
        dma((3, 2, 2, 2)),
        dma((3, 4)),
        dma((3, 4)),
        pltpu.SemaphoreType.REGULAR,
    ]
    hbm = pl.BlockSpec(memory_space=pltpu.HBM)
    vm_spec = pl.BlockSpec(memory_space=pltpu.VMEM)
    return pl.pallas_call(
        kernel,
        out_shape=[
            pltpu.VMEM((128, 128), F32),
            pltpu.VMEM((128, 256), F32),
        ],
        in_specs=[hbm] * 8,
        out_specs=[vm_spec, vm_spec],
        scratch_shapes=scratch,
        compiler_params=pltpu.CompilerParams(
            collective_id=0, has_side_effects=True, vmem_limit_bytes=60 * 1024 * 1024
        ),
        cost_estimate=pl.CostEstimate(flops=3_000_000_000, bytes_accessed=5_000_000, transcendentals=0),
    )(*args)


def solution(mesh):
    placed = (
        P("pole", None, "leaf", None),
        P("pole", None, None, "leaf"),
        P("pole", None, None, "leaf"),
        P("pole", None, None, "leaf"),
        P("pole", None, None, "leaf"),
        P(),
        P(),
        P("pole", None),
    )
    return jax.shard_map(
        local,
        mesh=mesh,
        in_specs=placed,
        out_specs=(P("pole", "leaf"), P("pole", "leaf")),
        check_vma=False,
    )
```
